32 devices in a mesh: section: 2 (over core), replica: 4 (over y, x), shard: 4 (over z).
Axes of the slice: x: 2, y: 2, z: 4, core: 2. Of those that a mesh axis runs over, the one named last changes fastest.
Arguments:
- boundary: bfloat16 [2, 2, 4, 1024, 1600], P('section', None, 'replica', 'shard'), may hold values from -6 to 6
- segments: int32 [2, 4, 1024], P(None, 'replica'), may hold values from 0 to 2, never falling along the last dimension, each value on 1 to 768 neighbouring positions
- attn_weight: bfloat16 [2, 1600, 4800], P('section', 'shard'), may hold values from -0.15625 to 0.15625
- proj_weight: bfloat16 [2, 1600, 1600], P('section', 'shard'), may hold values from -0.625 to 0.625
- fc_in_weight: bfloat16 [2, 1600, 6400], P('section', 'shard'), may hold values from -0.15625 to 0.15625
- fc_out_weight: bfloat16 [2, 6400, 1600], P('section', 'shard'), may hold values from -0.078125 to 0.078125
- norm_gains: float32 [2, 2, 1600], P('section'), may hold values from 0.5 to 1.5
- vector_bias: float32 [2, 6, 1600], P('section'), may hold values from -3 to 3
- fc_in_bias: float32 [2, 6400], P('section'), may hold values from -3 to 3
Outputs:
- edge: float32 [2, 2, 4, 1024, 1600], P('section', None, 'replica', 'shard')
- attn_weight_grad: float32 [2, 1600, 4800], P('section', 'shard')
- proj_weight_grad: float32 [2, 1600, 1600], P('section', 'shard')
- fc_in_weight_grad: float32 [2, 1600, 6400], P('section', 'shard')
- fc_out_weight_grad: float32 [2, 6400, 1600], P('section', 'shard')
- norm_gains_grad: float32 [2, 2, 1600], P('section')
- vector_bias_grad: float32 [2, 6, 1600], P('section')
- fc_in_bias_grad: float32 [2, 6400], P('section')
The draws below stay inside these ranges and needn't reach their ends.
Inputs may be any that keep to these rules, and one draw needn't show every extreme that they name: `segments`: each sequence holds three documents numbered 0, 1, 2 in order, none empty; the longest has exactly 768 tokens.
All inputs are finite; a program needn't handle non-finite values.
Results may differ from the reference program's by a relative error of at most 0.025.
Values may be sent and summed in bfloat16 or wider, within the bound.
No kernel may reach another device: no remote copies, remote signals or barrier semaphores. Data moves between devices by JAX's collectives and lax.ppermute only.
A program may use at most 448 MiB of HBM per device.

```python
import math
import jax
import jax.numpy as jnp
import numpy as np
from jax import lax

D = 1600
HEADS = 25
HEAD = 64
FF = 6400
LEN = 1024
MB = 2
LAYERS = 2
SEQS = 4
SEG_MOST = 768


def block_levels(rng, extent, shards, smallest, largest):
    level, own = 1.0, jax.random.fold_in(rng, 6)
    for position, shards_of in shards:
        heights = jnp.exp(jax.random.uniform(jax.random.fold_in(own, position), (shards_of,), jnp.float32, smallest / len(shards), largest / len(shards)))
        level = level * jnp.repeat(heights, extent[position] // shards_of).reshape([-1 if axis == position else 1 for axis in range(len(extent))])
    return level


def profile(number_of, total, most, lean):
    weights = [(1 << 20) // math.isqrt(standing ** lean) + 1 for standing in range(2, number_of + 1)]
    spare, holding = total - most - (number_of - 1), [1] * (number_of - 1)
    while spare > 0:
        movable = [i for i in range(number_of - 1) if holding[i] < most]
        whole, budget = sum([weights[i] for i in movable]), spare
        for i in movable:
            addition = min(most - holding[i], max(1, budget * weights[i] // whole), spare)
            holding[i] = holding[i] + addition
            spare = spare - addition
    return np.array([most] + holding)


def uneven_parts(key, number_of, total, bound, skew):
    if number_of == 2:
        one = jax.random.randint(key, (), max(1, total - bound), min(bound, total - 1) + 1)
        return jnp.stack([one, total - one])
    tallies = jnp.asarray(profile(number_of, total, bound, skew), jnp.int32)
    pairs = (number_of - 1) // 2
    donor, taker = tallies[1:1 + 2 * pairs:2], tallies[2:2 + 2 * pairs:2]
    room = jnp.minimum(donor - 1, bound - taker)
    shifted = jax.random.randint(jax.random.fold_in(key, 1), (pairs,), 0, 1 << 20) % (room + 1)
    tallies = tallies.at[1:1 + 2 * pairs:2].set(donor - shifted).at[2:2 + 2 * pairs:2].set(taker + shifted)
    return tallies[jax.random.permutation(jax.random.fold_in(key, 2), number_of)]


def scatter_about(key, shape, deviation, reach, split=(), held_as=jnp.bfloat16):
    level = block_levels(key, shape, split, -0.22, 0.18) if split else 1.0
    result = jax.random.normal(key, shape, jnp.float32) * deviation * level
    return jnp.minimum(jnp.maximum(result, -reach), reach).astype(held_as)


def setup_inputs(seed: int = 0) -> dict:
    key_list = jax.random.split(jax.random.key(seed), 10)
    return {
        "boundary": scatter_about(key_list[0], (LAYERS, MB, SEQS, LEN, D), 1.0, 6.0, ((0, 2), (2, 4), (3, 4))),
        "segments": jax.vmap(lambda own: jnp.searchsorted(jnp.cumsum(uneven_parts(own, 3, LEN, SEG_MOST, 0)), jnp.arange(LEN), side="right"))(jax.random.split(key_list[1], MB * SEQS)).reshape((MB, SEQS, LEN)).astype(jnp.int32),
        "attn_weight": scatter_about(key_list[2], (LAYERS, D, 3 * D), D ** -0.5, 0.15625, ((0, 2), (1, 4))),
        "proj_weight": scatter_about(key_list[3], (LAYERS, D, D), (D // 16) ** -0.5, 0.625, ((0, 2), (1, 4))),
        "fc_in_weight": scatter_about(key_list[4], (LAYERS, D, FF), D ** -0.5, 0.15625, ((0, 2), (1, 4))),
        "fc_out_weight": scatter_about(key_list[5], (LAYERS, FF, D), FF ** -0.5, 0.078125, ((0, 2), (1, 4))),
        "norm_gains": jnp.clip(1.0 + 0.1 * jax.random.normal(key_list[6], (LAYERS, 2, D), jnp.float32), 0.5, 1.5),
        "vector_bias": scatter_about(key_list[7], (LAYERS, 6, D), 0.5, 3.0, ((0, 2),), jnp.float32),
        "fc_in_bias": scatter_about(key_list[8], (LAYERS, FF), 0.5, 3.0, ((0, 2),), jnp.float32),
    }


@jax.custom_vjp
def low(v):
    return lax.optimization_barrier(v.astype(jnp.bfloat16)).astype(jnp.float32)

@jax.custom_vjp
def low_back(v):
    return v

def low_keep(v):
    return (low(v), None)

def low_pass(kept, grad):
    return (grad,)

def back_keep(v):
    return (v, None)

def back_low(kept, grad):
    return (low(grad),)
low.defvjp(low_keep, low_pass)
low_back.defvjp(back_keep, back_low)
EPSILON = 1e-05
MASKED = -1e+30

def product(left, right):
    return jnp.dot(left, right, precision=lax.Precision.HIGHEST, preferred_element_type=jnp.float32)

def layer_norm(value, gain, shift):
    centred = value - lax.optimization_barrier(jnp.mean(value, axis=-1, keepdims=True))
    variance = lax.optimization_barrier(jnp.mean(centred * centred, axis=-1, keepdims=True))
    return centred * lax.rsqrt(variance + EPSILON) * gain + shift

def attention(query, keys, values, segment_ids):
    length = query.shape[0]
    block = min(512, length)
    scale = HEAD ** (-0.5)
    places = jnp.arange(length, dtype=jnp.int32)

    def one_block(index):
        start = (index * block).astype(jnp.int32)
        rows = lax.dynamic_slice_in_dim(query, start, block, 0)
        row_ids = lax.dynamic_slice_in_dim(segment_ids, start, block, 0)
        row_places = start + jnp.arange(block, dtype=jnp.int32)
        raw = jnp.einsum('qhe,khe->hqk', rows, keys, precision=lax.Precision.HIGHEST)
        scores = low_back(raw * scale)
        mask = (row_ids[:, None] == segment_ids[None, :]) & (places[None, :] <= row_places[:, None])
        scores = jnp.where(mask[None], scores, MASKED)
        logsum = jax.nn.logsumexp(scores, axis=-1, keepdims=True)
        weights = jnp.exp(scores - logsum)
        return jnp.einsum('hqk,khe->qhe', low(weights), values, precision=lax.Precision.HIGHEST)
    blocks = lax.map(jax.checkpoint(one_block), jnp.arange(length // block, dtype=jnp.int32))
    return blocks.reshape(length, HEADS * HEAD)

def layer_apply(hidden, segment_ids, w_attn, w_proj, w_in, w_out, gains, biases, hid_bias):
    length, width = hidden.shape
    normed = low(layer_norm(hidden, gains[0], biases[0]))
    mixed = product(normed, w_attn)
    query = low(low_back(mixed[:, :width] + biases[1]))
    keys = low(low_back(mixed[:, width:2 * width]))
    values = low(low_back(mixed[:, 2 * width:] + biases[2]))
    shape = (length, HEADS, HEAD)
    attended = attention(query.reshape(shape), keys.reshape(shape), values.reshape(shape), segment_ids)
    attended = low(low_back(attended))
    middle = hidden + low_back(product(attended, w_proj) + biases[3])
    normed_two = low(layer_norm(middle, gains[1], biases[4]))
    pre = low_back(product(normed_two, w_in) + hid_bias)
    activated = low(jax.nn.gelu(pre, approximate=True))
    return middle + low_back(product(activated, w_out) + biases[5])

def forward(inputs, segment_ids, w_attn, w_proj, w_in, w_out, gains, biases, hid_bias):

    def one_sequence(pair):
        hidden, ids = pair
        passed = layer_apply(hidden, ids, w_attn[0], w_proj[0], w_in[0], w_out[0], gains[0], biases[0], hid_bias[0])
        passed = low(low_back(passed))
        return layer_apply(passed, ids, w_attn[1], w_proj[1], w_in[1], w_out[1], gains[1], biases[1], hid_bias[1])
    return lax.map(jax.checkpoint(one_sequence), (inputs, segment_ids))

def reference(boundary, segments, attn_weight, proj_weight, fc_in_weight, fc_out_weight, norm_gains, vector_bias, fc_in_bias):
    whole = boundary.astype(jnp.float32)
    block_in = whole[0].reshape(MB * SEQS, LEN, D)
    cotangent = whole[1].reshape(MB * SEQS, LEN, D)
    ids = segments.reshape(MB * SEQS, LEN)
    params = (attn_weight.astype(jnp.float32), proj_weight.astype(jnp.float32), fc_in_weight.astype(jnp.float32), fc_out_weight.astype(jnp.float32), norm_gains.astype(jnp.float32), vector_bias.astype(jnp.float32), fc_in_bias.astype(jnp.float32))

    def wrapped(inputs, w_attn, w_proj, w_in, w_out, gains, biases, hid_bias):
        return forward(inputs, ids, w_attn, w_proj, w_in, w_out, gains, biases, hid_bias)
    outputs, pullback = jax.vjp(wrapped, block_in, *params)
    grads = pullback(cotangent)
    edge = jnp.stack([grads[0], outputs]).reshape(LAYERS, MB, SEQS, LEN, D)
    return (edge, grads[1], grads[2], grads[3], grads[4], grads[5], grads[6], grads[7])
```

```python
from functools import partial

import jax
import jax.numpy as jnp
from jax import lax
from jax.experimental import pallas as pl
from jax.experimental.pallas import tpu as pltpu
from jax.sharding import Mesh, PartitionSpec as P

HEADS = 25
HEAD = 64
EPSILON = 1e-05
MASKED = -1e30
BF = jnp.bfloat16
F32 = jnp.float32
SWAP = [(0, 1), (1, 0)]
SIDE = [(0, 1), (1, 0), (2, 3), (3, 2)]
ACROSS = [(0, 2), (2, 0), (1, 3), (3, 1)]
CORNER = [(0, 3), (3, 0), (1, 2), (2, 1)]


def dot(left, right, contract):
    return lax.dot_general(
        left, right, ((contract[:1], contract[1:]), ((), ())), preferred_element_type=F32
    )


def norm_stats(value):
    centred = value - jnp.mean(value, axis=-1, keepdims=True)
    variance = jnp.mean(centred * centred, axis=-1, keepdims=True)
    inverse = lax.rsqrt(variance + EPSILON)
    return centred * inverse, inverse


def norm_back(grad, value, gain):
    unit, inverse = norm_stats(value)
    grad_unit = grad * gain
    mean_one = jnp.mean(grad_unit, axis=-1, keepdims=True)
    mean_two = jnp.mean(grad_unit * unit, axis=-1, keepdims=True)
    grad_value = inverse * (grad_unit - mean_one - unit * mean_two)
    return grad_value, jnp.sum(grad * unit, axis=0), jnp.sum(grad, axis=0)


def gelu_pair(x):
    c = 0.7978845608028654
    square = x * x
    th = jnp.tanh(c * x * (1.0 + 0.044715 * square))
    value = 0.5 * x * (1.0 + th)
    slope = 0.5 * (1.0 + th) + 0.5 * x * (1.0 - th * th) * c * (1.0 + 3 * 0.044715 * square)
    return value, slope


def spots(chunk, piece, block, n, teams):
    order = ((0, 2, 1, 3), (0, 1, 2, 3))[chunk]
    return [
        (index * n, order[piece * (block // n) + index], chunk * n) for index in range(block // n)
    ]


def attend_kernel(grouped, q_ref, k_ref, v_ref, bias_ref, *out_refs):
    *outs, lse_ref = out_refs
    length = q_ref.shape[1]
    half = length // 2
    n = half // 4
    block = min(256, half)
    for chunk in range(2):
        extent = half * (chunk + 1)
        for piece in range(half // block):
            at = chunk * half + piece * block
            query = q_ref[:, at : at + block] * jnp.asarray(HEAD ** (-0.5), BF)
            scores = dot(k_ref[:, :extent], query, (0, 0)) + bias_ref[:extent, at : at + block]
            best = jnp.max(scores, axis=0, keepdims=True)
            weights = jnp.exp(scores - best)
            total = jnp.sum(weights, axis=0, keepdims=True)
            out = dot(v_ref[:, :extent], weights.astype(BF), (1, 0)) / total
            out = out.astype(BF)
            if grouped:
                for here, owner, there in spots(chunk, piece, block, n, 4):
                    outs[owner][:, there : there + n] = out[:, here : here + n]
            else:
                outs[0][:, at : at + block] = out
            lse_ref[0, :, at : at + block] = best + jnp.log(total)


def attend_back_kernel(grouped, q_ref, k_ref, v_ref, bias_ref, lse_ref, *refs):
    *g_refs, dq_ref, dk_ref, dv_ref, keys, values = refs
    length = q_ref.shape[1]
    half = length // 2
    n = half // 4
    block = min(256, half)
    scale = HEAD ** (-0.5)
    keys[...] = jnp.zeros_like(keys)
    values[...] = jnp.zeros_like(values)
    for chunk in range(2):
        extent = half * (chunk + 1)
        for piece in range(half // block):
            at = chunk * half + piece * block
            query = q_ref[:, at : at + block] * jnp.asarray(scale, BF)
            if grouped:
                grad = jnp.concatenate(
                    [
                        g_refs[owner][:, there : there + n]
                        for _, owner, there in spots(chunk, piece, block, n, 4)
                    ],
                    axis=1,
                )
            else:
                grad = g_refs[0][:, at : at + block]
            scores = dot(k_ref[:, :extent], query, (0, 0)) + bias_ref[:extent, at : at + block]
            probs = jnp.exp(scores - lse_ref[0, :, at : at + block])
            inner = dot(v_ref[:, :extent], grad, (0, 0))
            rowdot = jnp.sum(probs * inner, axis=0, keepdims=True)
            dscore = (probs * (inner - rowdot)).astype(BF)
            values[:, :extent] += dot(grad, probs.astype(BF), (1, 1))
            keys[:, :extent] += dot(query, dscore, (1, 1))
            dq_ref[:, at : at + block] = (dot(k_ref[:, :extent], dscore, (1, 0)) * scale).astype(BF)
    dk_ref[...] = keys[...].astype(BF)
    dv_ref[...] = values[...].astype(BF)


def attend(mixed, bias, slots, grouped):
    length = mixed.shape[1]
    part = lambda first: pl.BlockSpec((HEAD, length), lambda h: (first + h, 0))
    whole = pl.BlockSpec((length, length), lambda h: (0, 0))
    count, span = (4, length // 4) if grouped else (1, length)
    *outs, lse = pl.pallas_call(
        partial(attend_kernel, grouped),
        grid=(slots,),
        in_specs=[part(0), part(slots), part(2 * slots), whole],
        out_specs=[pl.BlockSpec((HEAD, span), lambda h: (h, 0))] * count
        + [pl.BlockSpec((1, 1, length), lambda h: (h, 0, 0))],
        out_shape=[jax.ShapeDtypeStruct((slots * HEAD, span), BF)] * count
        + [jax.ShapeDtypeStruct((slots, 1, length), F32)],
        compiler_params=pltpu.CompilerParams(vmem_limit_bytes=40 * 2**20),
        cost_estimate=pl.CostEstimate(
            flops=3 * slots * length * length * HEAD,
            bytes_accessed=4 * length * length + 8 * slots * HEAD * length,
            transcendentals=slots * length * length,
        ),
    )(mixed, mixed, mixed, bias)
    return outs, lse


def attend_back(mixed, grads, bias, lse, slots, grouped):
    length = mixed.shape[1]
    part = lambda first: pl.BlockSpec((HEAD, length), lambda h: (first + h, 0))
    whole = pl.BlockSpec((length, length), lambda h: (0, 0))
    one = jax.ShapeDtypeStruct((slots * HEAD, length), BF)
    count, span = (4, length // 4) if grouped else (1, length)
    return pl.pallas_call(
        partial(attend_back_kernel, grouped),
        grid=(slots,),
        in_specs=[
            part(0),
            part(slots),
            part(2 * slots),
            whole,
            pl.BlockSpec((1, 1, length), lambda h: (h, 0, 0)),
        ]
        + [pl.BlockSpec((HEAD, span), lambda h: (h, 0))] * count,
        out_specs=[part(0), part(0), part(0)],
        out_shape=[one, one, one],
        scratch_shapes=[pltpu.VMEM((HEAD, length), F32), pltpu.VMEM((HEAD, length), F32)],
        compiler_params=pltpu.CompilerParams(vmem_limit_bytes=40 * 2**20),
        cost_estimate=pl.CostEstimate(
            flops=8 * slots * length * length * HEAD,
            bytes_accessed=4 * length * length + 14 * slots * HEAD * length,
            transcendentals=slots * length * length,
        ),
    )(mixed, mixed, mixed, bias, lse, *grads)


TOPS = (0, 2, 1, 3)
LOWS = (0, 1, 2, 3)


def kernel_call(kernel, member, inputs, outputs, scratch=()):
    count = len(inputs)
    size = sum(x.size * x.dtype.itemsize for x in inputs)
    size += sum(x.size * x.dtype.itemsize for x in outputs)
    return pl.pallas_call(
        kernel,
        in_specs=[pl.BlockSpec(memory_space=pltpu.SMEM)]
        + [pl.BlockSpec(memory_space=pltpu.VMEM)] * count,
        out_specs=[pl.BlockSpec(memory_space=pltpu.VMEM)] * len(outputs),
        out_shape=outputs,
        scratch_shapes=list(scratch),
        compiler_params=pltpu.CompilerParams(vmem_limit_bytes=48 * 2**20),
        cost_estimate=pl.CostEstimate(flops=0, bytes_accessed=size, transcendentals=0),
    )(member.reshape(1), *inputs)


def slab_places(member, rows, step, slab):
    found = []
    for part, order in enumerate((TOPS, LOWS)):
        for turn in order:
            owner = member ^ turn
            for block in (2 * part, 2 * part + 1):
                found.append((owner, block * rows + owner * step))
    return found


def sort_heads_kernel(slots, rows, step, slab, member_ref, *refs):
    *got, out_ref, whole = refs
    member = member_ref[0]
    width = whole.shape[0]
    high = slots * HEAD
    for turn in range(4):
        owner = member ^ turn
        at = jnp.minimum(owner * high, width - high)
        spare = (owner * high - at) // HEAD
        if turn == 0:
            pass
        for slot in range(slots):

            @pl.when(slot >= spare)
            def _(turn=turn, slot=slot, at=at):
                to = pl.multiple_of(at + slot * HEAD, HEAD)
                whole[pl.ds(to, HEAD), :] = got[turn][slot * HEAD : (slot + 1) * HEAD, :]

    line = lax.broadcasted_iota(jnp.int32, (slab, 1), 0)
    for index, (owner, at) in enumerate(slab_places(member, rows, step, slab)):
        rows_here = whole[pl.ds(pl.multiple_of(at, 16), slab), :]
        keep = (line < step) | (owner == 3)
        out_ref[index * slab : (index + 1) * slab, :] = jnp.where(
            keep, rows_here, jnp.zeros_like(rows_here)
        )


def split_heads_kernel(slots, rows, step, slab, member_ref, value_ref, *refs):
    *outs, whole = refs
    member = member_ref[0]
    width = whole.shape[0]
    high = slots * HEAD
    for index, (owner, at) in enumerate(slab_places(member, rows, step, slab)):
        first = index * slab
        whole[pl.ds(pl.multiple_of(at, 16), step), :] = value_ref[first : first + step, :]

        @pl.when(owner == 3)
        def _(first=first, at=at):
            to = pl.multiple_of(at + step, 16)
            whole[pl.ds(to, slab - step), :] = value_ref[first + step : first + slab, :]

    for turn in range(4):
        owner = member ^ turn
        at = jnp.minimum(owner * high, width - high)
        spare = owner * high - at
        line = lax.broadcasted_iota(jnp.int32, (high, 1), 0)
        rows_here = whole[pl.ds(pl.multiple_of(at, HEAD), high), :]
        outs[turn][...] = jnp.where(line >= spare, rows_here, jnp.zeros_like(rows_here))


def member_rows(refs, member, owner, cut, rows):
    turn = member ^ owner
    twin = (turn & 1) * 2 + turn // 2
    found = []
    for ref in refs:
        top = ref[pl.ds(pl.multiple_of(twin * cut, 16), cut), :]
        low = ref[pl.ds(pl.multiple_of(4 * cut + turn * (rows - cut), 16), rows - cut), :]
        found.append((top.astype(F32), low.astype(F32)))
    return found


def finish_attn_kernel(slots, cut, member_ref, left_ref, right_ref, out_ref):
    member = member_ref[0]
    rows = out_ref.shape[0]
    width = out_ref.shape[1] // 3
    high = slots * HEAD
    for owner in range(4):
        start = min(owner * high, width - high)
        spare = owner * high - start
        (left, right) = member_rows((left_ref, right_ref), member, owner, cut, rows)
        for lines, place in ((0, slice(0, cut)), (1, slice(cut, rows))):
            both = jnp.concatenate([left[lines], right[lines]], axis=1)
            for third in range(3):
                to = third * width + start + spare
                out_ref[place, to : to + high - spare] = both[
                    :, third * high + spare : (third + 1) * high
                ]


def finish_proj_kernel(step, slab, cut, member_ref, left_ref, right_ref, out_ref):
    member = member_ref[0]
    rows = out_ref.shape[0]
    for owner in range(4):
        size = slab if owner == 3 else step
        (left, right) = member_rows((left_ref, right_ref), member, owner, cut, slab)
        both = [jnp.concatenate([left[i], right[i]], axis=1) for i in range(2)]
        whole = jnp.concatenate(both)
        out_ref[owner * step : owner * step + size, :] = whole[:size]


def finish_in_kernel(cut, member_ref, value_ref, out_ref):
    member = member_ref[0]
    rows = out_ref.shape[0]
    part = out_ref.shape[1] // 16
    for owner in range(4):
        ((top, low),) = member_rows((value_ref,), member, owner, cut, rows)
        for block in range(4):
            to = (block * 4 + owner) * part
            out_ref[:cut, to : to + part] = top[:, block * part : (block + 1) * part]
            out_ref[cut:, to : to + part] = low[:, block * part : (block + 1) * part]


def finish_out_kernel(cut, member_ref, value_ref, out_ref):
    member = member_ref[0]
    rows = out_ref.shape[0] // 4
    for owner in range(4):
        ((top, low),) = member_rows((value_ref,), member, owner, cut, rows)
        out_ref[owner * rows : owner * rows + cut, :] = top
        out_ref[owner * rows + cut : (owner + 1) * rows, :] = low


def tie(value, *others):
    return lax.optimization_barrier((value, others))[0]


def body(
    replicas,
    shards,
    boundary,
    segments,
    attn_weight,
    proj_weight,
    fc_in_weight,
    fc_out_weight,
    norm_gains,
    vector_bias,
    fc_in_bias,
):
    sub = shards // replicas
    team = replicas * sub
    fast = replicas == 4 and sub == 1
    team_axes = ("replica", "sub")
    row_axes = ("seq", "sub")
    chip_axes = ("replica", "seq", "sub")
    section = lax.axis_index("section")
    first = section == 0
    member = lax.axis_index(team_axes)
    local = boundary.shape[3]
    width = boundary.shape[4]
    hidden = fc_in_bias.shape[1]
    n = local // 2
    length = segments.shape[2]
    half = length // 2
    slots = -(-HEADS // team)
    heads_width = slots * HEAD
    hid = hidden // team
    cols = width // team

    def head_start(index):
        return jnp.minimum(index * slots, HEADS - slots)

    def spare_heads(index):
        return min(max(index * slots - (HEADS - slots), 0), slots)

    start = head_start(member) * HEAD

    def cross(value, pairs=SWAP):
        return lax.ppermute(value, "section", pairs)

    def side(value):
        return lax.ppermute(value, "replica", SIDE)

    def across(value):
        return lax.ppermute(value, "replica", ACROSS)

    def corner(value):
        return lax.ppermute(value, "replica", CORNER)

    def pick(a, b):
        return jnp.where(first, a, b)

    def flat(p, z):
        return p * shards + z

    rounds = []
    for turn in range(2):
        pairs = []
        for p in range(replicas):
            for z in range(shards):
                slot = z // (shards // 2)
                h = turn if slot == 0 else 1 - turn
                j = 2 * (z % (shards // 2)) + h
                target = flat(j // sub, p * sub + j % sub)
                pairs.append((flat(p, z), target))
        rounds.append(pairs)
    place = lax.axis_index(row_axes)
    early = place < shards // 2
    even = member % 2 == 0

    def to_team(value):
        top, low = value[:n], value[n:]
        one = lax.ppermute(jnp.where(early, top, low), chip_axes, rounds[0])
        two = lax.ppermute(jnp.where(early, low, top), chip_axes, rounds[1])
        return jnp.concatenate([jnp.where(even, one, two), jnp.where(even, two, one)])

    def from_team(value):
        top, low = value[:n], value[n:]
        one = lax.ppermute(
            jnp.where(even, top, low), chip_axes, [(b, a) for a, b in rounds[0]]
        )
        two = lax.ppermute(
            jnp.where(even, low, top), chip_axes, [(b, a) for a, b in rounds[1]]
        )
        return jnp.concatenate([jnp.where(early, one, two), jnp.where(early, two, one)])

    if fast:
        order_a = [member, member ^ 2, member ^ 1, member ^ 3]
        order_b = [member, member ^ 1, member ^ 2, member ^ 3]
    else:
        order_a = order_b = list(range(team))

    def gather(value, cut):
        a, b = value[:cut], value[cut:]
        if not fast:
            return jnp.concatenate(
                [
                    lax.all_gather(a, team_axes, axis=0, tiled=True),
                    lax.all_gather(b, team_axes, axis=0, tiled=True),
                ]
            )
        near_a, near_b = across(a), side(b)
        far_a = side(jnp.concatenate([a, near_a]))
        far_b = across(jnp.concatenate([b, near_b]))
        return jnp.concatenate([a, near_a, far_a, b, near_b, far_b])

    def scatter(value):
        middle_row = value.shape[0] // 2
        a, b = value[:middle_row], value[middle_row:]
        if not fast:
            return jnp.concatenate(
                [
                    lax.psum_scatter(a.astype(F32), team_axes, scatter_dimension=0, tiled=True),
                    lax.psum_scatter(b.astype(F32), team_axes, scatter_dimension=0, tiled=True),
                ]
            )
        m = middle_row // 4
        got_a, got_b = side(a[2 * m :]), across(b[2 * m :])
        sent_a = (a[m : 2 * m].astype(F32) + got_a[m:]).astype(BF)
        sent_b = (b[m : 2 * m].astype(F32) + got_b[m:]).astype(BF)
        last_a, last_b = across(sent_a), side(sent_b)
        sum_a = a[:m].astype(F32) + got_a[:m] + last_a
        sum_b = b[:m].astype(F32) + got_b[:m] + last_b
        return jnp.concatenate([sum_a, sum_b])

    if fast:
        rows = width // replicas
        slab = -(-rows // 64) * 16
        step = (rows - slab) // 3
        cut = (rows // 32) * 16
        wide = jax.ShapeDtypeStruct((16 * slab, 2 * n), BF)
        one = jax.ShapeDtypeStruct((heads_width, 2 * n), BF)
        scratch = [pltpu.VMEM((width, 2 * n), BF)]

    def heads_to_tokens(values):
        if fast:
            own, near, over, far = values
            got = [own, side(near), across(over), corner(far)]
            kernel = partial(sort_heads_kernel, slots, rows, step, slab)
            return kernel_call(kernel, member, got, [wide], scratch)[0]
        pieces = values[0].reshape(heads_width, 2, team, n).transpose(2, 0, 1, 3)
        got = lax.all_to_all(pieces, team_axes, 0, 0, tiled=True)
        got = got.reshape(team, heads_width, 2 * n)
        pieces = []
        for index in range(team):
            spare = spare_heads(index) * HEAD
            if spare < heads_width:
                pieces.append(got[index, spare:])
        return jnp.concatenate(pieces)

    def tokens_to_heads(value):
        if fast:
            kernel = partial(split_heads_kernel, slots, rows, step, slab)
            own, near, over, far = kernel_call(kernel, member, [value], [one] * 4, scratch)
            return [own, side(near), across(over), corner(far)]

        def of(index):
            return lax.dynamic_slice_in_dim(value, head_start(index) * HEAD, heads_width, 0)

        pieces = jnp.stack([of(index) for index in range(team)])
        got = lax.all_to_all(pieces, team_axes, 0, 0, tiled=True)
        got = got.reshape(team, heads_width, 2, n).transpose(1, 2, 0, 3)
        whole = got.reshape(heads_width, length)
        spare = member * slots - head_start(member)
        lines = lax.broadcasted_iota(jnp.int32, (heads_width, 1), 0)
        return [jnp.where(lines >= spare * HEAD, whole, jnp.zeros_like(whole))]

    def head_columns(weight):
        return [
            lax.dynamic_slice_in_dim(weight, third * width + start, heads_width, 1)
            for third in range(3)
        ]

    if fast:
        hid_part = hid // replicas
        own_attn = jnp.concatenate(head_columns(attn_weight[0]), axis=1)
        attn_half = own_attn.shape[1] // 2
        own_in = jnp.concatenate(
            [
                lax.dynamic_slice_in_dim(
                    fc_in_weight[0], block * hid + member * hid_part, hid_part, 1
                )
                for block in range(replicas)
            ],
            axis=1,
        )
        own_out = lax.dynamic_slice_in_dim(fc_out_weight[0], member * hid_part, hid_part, 0)

        def spread(own_0, own_1):
            got = cross(pick(own_1, own_0))
            return pick(own_0, got), pick(got, own_1)

        def full(piece):
            mine = lax.all_gather(piece, "seq", axis=0, tiled=True)
            other = cross(mine)
            return pick(mine, other), pick(other, mine)

        attn_pieces = spread(own_attn[:, :attn_half], own_attn[:, attn_half:])
        fc_pieces = spread(own_in, own_out)
        own_proj = lax.dynamic_slice_in_dim(proj_weight[0], member * step, slab, 0)

        def weights_whole():
            attn_0 = jnp.concatenate(full(attn_pieces[0]), axis=1)
            proj = lax.all_gather(own_proj, "seq", axis=0, tiled=True)
            proj = gather(proj, 2 * slab)
            other = cross(proj)
            fc_0 = full(fc_pieces[0])
            attn_1 = jnp.concatenate(full(attn_pieces[1]), axis=1)
            fc_1 = full(fc_pieces[1])
            return (attn_0, pick(proj, other), *fc_0), (attn_1, pick(other, proj), *fc_1)

        def hid_of(vector):
            return lax.dynamic_slice_in_dim(
                vector.reshape(replicas, replicas, hid_part), member, 1, 1
            ).reshape(hid)

        def hid_into(vector):
            zeros = jnp.zeros((replicas, replicas, hid_part), F32)
            return lax.dynamic_update_slice_in_dim(
                zeros, vector.reshape(replicas, 1, hid_part), member, 1
            ).reshape(hidden)

    else:

        def both(value):
            other = cross(value)
            return pick(value, other), pick(other, value)

        def weights_of(layer):
            def whole(weight):
                return lax.all_gather(both(weight[0])[layer], row_axes, axis=0, tiled=True)

            w_attn = jnp.concatenate(head_columns(whole(attn_weight)), axis=1)
            w_proj = whole(proj_weight)
            w_in = lax.dynamic_slice_in_dim(whole(fc_in_weight), member * hid, hid, 1)
            w_out = lax.dynamic_slice_in_dim(whole(fc_out_weight), member * hid, hid, 0)
            return w_attn, w_proj, w_in, w_out

        def weights_whole():
            return weights_of(0), weights_of(1)

        def hid_of(vector):
            return lax.dynamic_slice_in_dim(vector, member * hid, hid, 0)

        def hid_into(vector):
            return lax.dynamic_update_slice_in_dim(
                jnp.zeros((hidden,), F32), vector, member * hid, 0
            )

    def heads_into(vector):
        return lax.dynamic_update_slice_in_dim(jnp.zeros((width,), F32), vector, start, 0)

    block_0, block_1 = boundary[0, 0, 0], boundary[0, 1, 0]
    kept = pick(block_0, block_1)
    got = cross(pick(block_1, block_0))
    source = to_team(pick(kept, got))
    cotangent = pick(got, kept)
    vectors = jnp.concatenate([norm_gains[0].ravel(), vector_bias[0].ravel(), fc_in_bias[0]])
    other_vectors = cross(vectors)
    vectors = (pick(vectors, other_vectors), pick(other_vectors, vectors))

    ids = lax.dynamic_index_in_dim(segments, section, 0, keepdims=False)[0]
    swapped = [
        (flat(p, z * sub + k), flat(z, p * sub + k))
        for p in range(replicas)
        for z in range(replicas)
        for k in range(sub)
    ]
    ids = lax.ppermute(ids, chip_axes, swapped).reshape(2, team, n)
    places, names = [], []
    for chunk, order in enumerate((order_a, order_b)):
        for index in order:
            places.append(chunk * half + index * n + jnp.arange(n, dtype=jnp.int32))
            names.append(lax.dynamic_index_in_dim(ids[chunk], index, 0, keepdims=False))
    places, names = jnp.concatenate(places), jnp.concatenate(names)
    allowed = (names[:, None] == names[None, :]) & (places[:, None] <= places[None, :])
    bias = jnp.where(allowed, 0.0, MASKED).astype(F32)

    def parameters(layer):
        vector = vectors[layer]
        gains = vector[: 2 * width].reshape(2, width)
        biases = vector[2 * width : 8 * width].reshape(6, width)
        hid_bias = hid_of(vector[8 * width :])
        query_bias = lax.dynamic_slice_in_dim(biases[1], start, heads_width, 0)
        value_bias = lax.dynamic_slice_in_dim(biases[2], start, heads_width, 0)
        mixed_bias = jnp.concatenate([query_bias, jnp.zeros_like(query_bias), value_bias])
        return gains, biases, hid_bias, mixed_bias

    def forward(layer, value, weights):
        w_attn, w_proj, w_in, w_out = weights
        gains, biases, hid_bias, mixed_bias = parameters(layer)
        normed = (norm_stats(value)[0] * gains[0] + biases[0]).astype(BF)
        normed = gather(normed, n)
        mixed = (dot(w_attn, normed, (0, 1)) + mixed_bias[:, None]).astype(BF)
        attended, lse = attend(mixed, bias, slots, fast)
        attended = heads_to_tokens(attended)
        middle = value + dot(attended, w_proj, (0, 0)) + biases[3]
        normed_two = (norm_stats(middle)[0] * gains[1] + biases[4]).astype(BF)
        normed_two = gather(normed_two, n)
        activated, slope = gelu_pair(dot(normed_two, w_in, (1, 0)) + hid_bias)
        activated, slope = activated.astype(BF), slope.astype(BF)
        out = middle + scatter(dot(activated, w_out, (1, 0)).astype(BF)) + biases[5]
        return out, (value, normed, mixed, lse, attended, middle, normed_two, activated, slope)

    ones = lax.optimization_barrier(jnp.ones((16, length), BF))

    def backward(layer, grad_out, kept, weights, waiting):
        value, normed, mixed, lse, attended, middle, normed_two, activated, slope = kept
        w_attn, w_proj, w_in, w_out = weights
        gains = parameters(layer)[0]
        grad_low = grad_out.astype(BF)
        low_sum = jnp.sum(grad_low.astype(F32), axis=0)
        grad_low = tie(gather(grad_low, n), waiting)
        grad_pre = (dot(grad_low, w_out, (1, 1)) * slope).astype(BF)
        grad_two = scatter(dot(grad_pre, w_in, (1, 1)).astype(BF))
        fc_pair = split_pair(dot(normed_two, grad_pre, (0, 0)), dot(activated, grad_low, (0, 0)))
        grad_two = tie(grad_two, fc_pair)
        hid_sum = dot(ones, grad_pre, (1, 0))[0]
        grad_norm, gain_two, shift_two = norm_back(grad_two, middle, gains[1])
        grad_middle = grad_out + grad_norm
        grad_branch = grad_middle.astype(BF)
        branch_sum = jnp.sum(grad_branch.astype(F32), axis=0)
        grad_attended = dot(w_proj, grad_branch, (1, 1)).astype(BF)
        grad_attended = tokens_to_heads(grad_attended)
        fc_total = join_pair(fc_pair)
        most = width // 2
        proj_pair = split_pair(
            dot(attended, grad_branch[:, :most], (1, 0)),
            dot(attended, grad_branch[:, most:], (1, 0)),
        )
        grad_attended = tie(grad_attended, fc_total, proj_pair)
        grad_q, grad_k, grad_v = attend_back(mixed, grad_attended, bias, lse, slots, fast)
        grad_mixed = jnp.concatenate([grad_q, grad_k, grad_v])
        grad_one = scatter(dot(grad_mixed, w_attn, (0, 1)).astype(BF))
        proj_total = join_pair(proj_pair)
        most = grad_mixed.shape[0] // 2
        attn_pair = split_pair(
            dot(normed, grad_mixed[:most], (0, 1)), dot(normed, grad_mixed[most:], (0, 1))
        )
        grad_one = tie(grad_one, attn_pair, proj_total)
        query_sum = jnp.sum(grad_q.astype(F32), axis=1)
        value_sum = jnp.sum(grad_v.astype(F32), axis=1)
        grad_norm, gain_one, shift_one = norm_back(grad_one, value, gains[0])
        grad_in = grad_middle + grad_norm
        small = jnp.concatenate(
            [
                gain_one,
                gain_two,
                shift_one,
                heads_into(query_sum),
                heads_into(value_sum),
                branch_sum,
                shift_two,
                low_sum,
                hid_into(hid_sum),
            ]
        )
        return grad_in, small, fc_total, proj_total, join_pair(attn_pair)

    def split_pair(part_0, part_1):
        if not fast:
            return part_0.astype(BF), part_1.astype(BF)
        return pick(part_0, part_1), cross(pick(part_1, part_0).astype(BF))

    def join_pair(pair):
        if not fast:
            return pair
        return (pair[0] + pair[1]).astype(BF)

    if fast:

        def collect(layer, total, at):
            mine = lax.psum_scatter(total, "seq", scatter_dimension=0, tiled=True)
            mine = gather(mine, at)
            return mine, cross(mine, [(1 - layer, layer)])

        def finish(kernel, pairs, shape):
            (mine_0, other_0), (mine_1, other_1) = pairs
            left, right = pick(mine_0, other_1), pick(other_0, mine_1)
            out = jax.ShapeDtypeStruct(shape, F32)
            return kernel_call(kernel, member, [left, right], [out])[0]

        def finish_fc(pairs):
            (mine_0, other_0), (mine_1, other_1) = pairs
            left, right = pick(mine_0, other_1), pick(other_0, mine_1)
            w_in = kernel_call(
                partial(finish_in_kernel, cut),
                member,
                [left],
                [jax.ShapeDtypeStruct((rows, hidden), F32)],
            )[0]
            w_out = kernel_call(
                partial(finish_out_kernel, cut),
                member,
                [right],
                [jax.ShapeDtypeStruct((hid, width), F32)],
            )[0]
            return w_in, w_out

        def reduce_small(small):
            total = pick(small[0], small[1]) + cross(pick(small[1], small[0]))
            total = total.reshape(-1, 128)
            for axis, pairs in (
                ("replica", SIDE),
                ("replica", ACROSS),
                ("seq", SIDE),
                ("seq", CORNER),
            ):
                total = total + lax.ppermute(total, axis, pairs)
            return total.reshape(-1)

    values = source.astype(F32)
    weights = weights_whole()
    passed, kept_0 = forward(0, values, weights[0])
    out, kept_1 = forward(1, passed.astype(BF).astype(F32), weights[1])
    cotangent = to_team(tie(cotangent, kept_0[1])).astype(F32)
    grad, small_1, fc_1, proj_1, attn_1 = backward(1, cotangent, kept_1, weights[1], ())
    grad = grad.astype(BF).astype(F32)
    grad, small_0, fc_0, proj_0, attn_0 = backward(0, grad, kept_0, weights[0], (attn_1,))
    out = from_team(out.astype(BF))
    grad = from_team(grad.astype(BF))
    got_out, got_grad = cross(out, [(0, 1)]), cross(grad, [(1, 0)])
    edge = jnp.stack([pick(grad, got_out), pick(got_grad, out)]).astype(F32)
    edge = edge.reshape(1, 2, 1, local, width)
    if fast:
        fc = [collect(layer, total, cut) for layer, total in enumerate((fc_0, fc_1))]
        attn = [collect(layer, total, cut) for layer, total in enumerate((attn_0, attn_1))]
        proj_cut = (slab // 32) * 16
        proj = [
            collect(layer, scatter(total).astype(BF), proj_cut)
            for layer, total in enumerate((proj_0, proj_1))
        ]
        in_sum, out_sum = finish_fc(fc)
        proj_sum = finish(partial(finish_proj_kernel, step, slab, proj_cut), proj, (rows, width))
        attn_sum = finish(partial(finish_attn_kernel, slots, cut), attn, (rows, 3 * width))
        small = reduce_small((small_0, small_1))
    else:

        def summed(make, after):
            parts = [tie(make(layer), after) for layer in range(2)]
            mine = pick(parts[0], parts[1]) + cross(pick(parts[1], parts[0]))
            mine = lax.psum_scatter(mine, row_axes, scatter_dimension=0, tiled=True)
            return lax.psum(mine.astype(F32), ("replica",))

        def attn_whole(layer):
            value = jnp.concatenate((attn_0, attn_1)[layer], axis=1)
            zeros = jnp.zeros((width, width), BF)
            parts = [value[:, i * heads_width : (i + 1) * heads_width] for i in range(3)]
            return jnp.concatenate(
                [lax.dynamic_update_slice_in_dim(zeros, x, start, 1) for x in parts], axis=1
            )

        def proj_whole(layer):
            return jnp.concatenate((proj_0, proj_1)[layer], axis=1)

        def in_whole(layer):
            zeros = jnp.zeros((width, hidden), BF)
            part = (fc_0, fc_1)[layer][0]
            return lax.dynamic_update_slice_in_dim(zeros, part, member * hid, 1)

        def out_whole(layer):
            zeros = jnp.zeros((hidden, width), BF)
            part = (fc_0, fc_1)[layer][1]
            return lax.dynamic_update_slice_in_dim(zeros, part, member * hid, 0)

        attn_sum = summed(attn_whole, edge)
        proj_sum = summed(proj_whole, attn_sum)
        in_sum = summed(in_whole, proj_sum)
        out_sum = summed(out_whole, in_sum)
        small = pick(small_0, small_1) + cross(pick(small_1, small_0))
        small = lax.psum(small, chip_axes)
    return (
        edge,
        attn_sum[None],
        proj_sum[None],
        in_sum[None],
        out_sum[None],
        small[: 2 * width].reshape(1, 2, width),
        small[2 * width : 8 * width].reshape(1, 6, width),
        small[8 * width :][None],
    )


def solution(mesh):
    sections, replicas, shards = (mesh.shape[name] for name in ("section", "replica", "shard"))
    split = Mesh(
        mesh.devices.reshape(sections, replicas, replicas, shards // replicas),
        ("section", "replica", "seq", "sub"),
    )
    rows = ("seq", "sub")
    return jax.shard_map(
        partial(body, replicas, shards),
        mesh=split,
        in_specs=(
            P("section", None, "replica", rows, None),
            P(None, "replica", None),
            P("section", rows, None),
            P("section", rows, None),
            P("section", rows, None),
            P("section", rows, None),
            P("section", None, None),
            P("section", None, None),
            P("section", None),
        ),
        out_specs=(
            P("section", None, "replica", rows, None),
            P("section", rows, None),
            P("section", rows, None),
            P("section", rows, None),
            P("section", rows, None),
            P("section", None, None),
            P("section", None, None),
            P("section", None),
        ),
        check_vma=False,
    )
```

```python
from functools import partial

import jax
import jax.numpy as jnp
from jax import lax
from jax.experimental import pallas as pl
from jax.experimental.pallas import tpu as pltpu
from jax.sharding import Mesh, PartitionSpec as P

HEADS = 25
HEAD = 64
EPSILON = 1e-05
MASKED = -1e30
BF = jnp.bfloat16
F32 = jnp.float32
SWAP = [(0, 1), (1, 0)]
SIDE = [(0, 1), (1, 0), (2, 3), (3, 2)]
ACROSS = [(0, 2), (2, 0), (1, 3), (3, 1)]
CORNER = [(0, 3), (3, 0), (1, 2), (2, 1)]


def dot(left, right, contract):
    return lax.dot_general(
        left, right, ((contract[:1], contract[1:]), ((), ())), preferred_element_type=F32
    )


def norm_stats(value, mask, width):
    mean = jnp.sum(value, axis=-1, keepdims=True) * (1.0 / width)
    centred = value - mean if mask is None else (value - mean) * mask
    variance = jnp.sum(centred * centred, axis=-1, keepdims=True) * (1.0 / width)
    inverse = lax.rsqrt(variance + EPSILON)
    return centred * inverse, inverse


def norm_back(grad, value, gain, mask, width):
    unit, inverse = norm_stats(value, mask, width)
    grad_unit = grad * gain
    mean_one = jnp.sum(grad_unit, axis=-1, keepdims=True) * (1.0 / width)
    mean_two = jnp.sum(grad_unit * unit, axis=-1, keepdims=True) * (1.0 / width)
    grad_value = inverse * (grad_unit - mean_one - unit * mean_two)
    if mask is not None:
        grad_value = grad_value * mask
    return grad_value, jnp.sum(grad * unit, axis=0), jnp.sum(grad, axis=0)


def gelu_pair(x):
    c = 0.7978845608028654
    square = x * x
    th = jnp.tanh(c * x * (1.0 + 0.044715 * square))
    value = 0.5 * x * (1.0 + th)
    slope = 0.5 * (1.0 + th) + 0.5 * x * (1.0 - th * th) * c * (1.0 + 3 * 0.044715 * square)
    return value, slope


def spots(chunk, piece, block, n, teams):
    order = ((0, 2, 1, 3), (0, 1, 2, 3))[chunk]
    return [
        (index * n, order[piece * (block // n) + index], chunk * n) for index in range(block // n)
    ]


def attend_kernel(grouped, q_ref, k_ref, v_ref, bias_ref, *out_refs):
    *outs, lse_ref = out_refs
    length = q_ref.shape[1]
    half = length // 2
    n = half // 4
    block = min(256, half)
    for chunk in range(2):
        extent = half * (chunk + 1)
        for piece in range(half // block):
            at = chunk * half + piece * block
            query = q_ref[:, at : at + block] * jnp.asarray(HEAD ** (-0.5), BF)
            scores = dot(k_ref[:, :extent], query, (0, 0)) + bias_ref[:extent, at : at + block]
            best = jnp.max(scores, axis=0, keepdims=True)
            weights = jnp.exp(scores - best)
            total = jnp.sum(weights, axis=0, keepdims=True)
            out = dot(v_ref[:, :extent], weights.astype(BF), (1, 0)) / total
            out = out.astype(BF)
            if grouped:
                for here, owner, there in spots(chunk, piece, block, n, 4):
                    outs[owner][:, there : there + n] = out[:, here : here + n]
            else:
                outs[0][:, at : at + block] = out
            lse_ref[0, :, at : at + block] = best + jnp.log(total)


def attend_back_kernel(grouped, q_ref, k_ref, v_ref, bias_ref, lse_ref, *refs):
    *g_refs, out_ref, keys, values = refs
    head = pl.program_id(0)
    slots = pl.num_programs(0)
    length = q_ref.shape[1]
    half = length // 2
    n = half // 4
    block = min(256, half)
    scale = HEAD ** (-0.5)
    keys[...] = jnp.zeros_like(keys)
    values[...] = jnp.zeros_like(values)
    for chunk in range(2):
        extent = half * (chunk + 1)
        for piece in range(half // block):
            at = chunk * half + piece * block
            query = q_ref[:, at : at + block] * jnp.asarray(scale, BF)
            if grouped:
                grad = jnp.concatenate(
                    [
                        g_refs[owner][:, there : there + n]
                        for _, owner, there in spots(chunk, piece, block, n, 4)
                    ],
                    axis=1,
                )
            else:
                grad = g_refs[0][:, at : at + block]
            scores = dot(k_ref[:, :extent], query, (0, 0)) + bias_ref[:extent, at : at + block]
            probs = jnp.exp(scores - lse_ref[0, :, at : at + block])
            inner = dot(v_ref[:, :extent], grad, (0, 0))
            rowdot = jnp.sum(probs * inner, axis=0, keepdims=True)
            dscore = (probs * (inner - rowdot)).astype(BF)
            values[:, :extent] += dot(grad, probs.astype(BF), (1, 1))
            keys[:, :extent] += dot(query, dscore, (1, 1))
            grad_query = (dot(k_ref[:, :extent], dscore, (1, 0)) * scale).astype(BF)
            out_ref[pl.ds(pl.multiple_of(head * HEAD, HEAD), HEAD), at : at + block] = grad_query
    key_rows = pl.ds(pl.multiple_of((slots + head) * HEAD, HEAD), HEAD)
    value_rows = pl.ds(pl.multiple_of((2 * slots + head) * HEAD, HEAD), HEAD)
    out_ref[key_rows, :] = keys[...].astype(BF)
    out_ref[value_rows, :] = values[...].astype(BF)

    @pl.when(head == 0)
    def _():
        used = 3 * HEAD * pl.num_programs(0)
        spare = out_ref.shape[0] % (3 * HEAD)
        if spare:
            rest = pl.ds(pl.multiple_of(used, HEAD), spare)
            out_ref[rest, :] = jnp.zeros((spare, length), BF)


def attend(mixed, bias, slots, grouped):
    length = mixed.shape[1]
    part = lambda first: pl.BlockSpec((HEAD, length), lambda h: (first + h, 0))
    whole = pl.BlockSpec((length, length), lambda h: (0, 0))
    count, span = (4, length // 4) if grouped else (1, length)
    *outs, lse = pl.pallas_call(
        partial(attend_kernel, grouped),
        grid=(slots,),
        in_specs=[part(0), part(slots), part(2 * slots), whole],
        out_specs=[pl.BlockSpec((HEAD, span), lambda h: (h, 0))] * count
        + [pl.BlockSpec((1, 1, length), lambda h: (h, 0, 0))],
        out_shape=[jax.ShapeDtypeStruct((slots * HEAD, span), BF)] * count
        + [jax.ShapeDtypeStruct((slots, 1, length), F32)],
        compiler_params=pltpu.CompilerParams(vmem_limit_bytes=40 * 2**20),
        cost_estimate=pl.CostEstimate(
            flops=42 * slots * length * length * HEAD,
            bytes_accessed=4 * length * length + 8 * slots * HEAD * length,
            transcendentals=slots * length * length,
        ),
    )(mixed, mixed, mixed, bias)
    return outs, lse


def attend_back(mixed, grads, bias, lse, slots, grouped):
    length = mixed.shape[1]
    part = lambda first: pl.BlockSpec((HEAD, length), lambda h: (first + h, 0))
    whole = pl.BlockSpec((length, length), lambda h: (0, 0))
    count, span = (4, length // 4) if grouped else (1, length)
    return pl.pallas_call(
        partial(attend_back_kernel, grouped),
        grid=(slots,),
        in_specs=[
            part(0),
            part(slots),
            part(2 * slots),
            whole,
            pl.BlockSpec((1, 1, length), lambda h: (h, 0, 0)),
        ]
        + [pl.BlockSpec((HEAD, span), lambda h: (h, 0))] * count,
        out_specs=pl.BlockSpec(mixed.shape, lambda h: (0, 0)),
        out_shape=jax.ShapeDtypeStruct(mixed.shape, BF),
        scratch_shapes=[pltpu.VMEM((HEAD, length), F32), pltpu.VMEM((HEAD, length), F32)],
        compiler_params=pltpu.CompilerParams(vmem_limit_bytes=40 * 2**20),
        cost_estimate=pl.CostEstimate(
            flops=48 * slots * length * length * HEAD,
            bytes_accessed=4 * length * length + 14 * slots * HEAD * length,
            transcendentals=slots * length * length,
        ),
    )(mixed, mixed, mixed, bias, lse, *grads)


TOPS = (0, 2, 1, 3)
LOWS = (0, 1, 2, 3)


def kernel_call(kernel, member, inputs, outputs, scratch=()):
    count = len(inputs)
    size = sum(x.size * x.dtype.itemsize for x in inputs)
    size += sum(x.size * x.dtype.itemsize for x in outputs)
    return pl.pallas_call(
        kernel,
        in_specs=[pl.BlockSpec(memory_space=pltpu.SMEM)]
        + [pl.BlockSpec(memory_space=pltpu.VMEM)] * count,
        out_specs=[pl.BlockSpec(memory_space=pltpu.VMEM)] * len(outputs),
        out_shape=outputs,
        scratch_shapes=list(scratch),
        compiler_params=pltpu.CompilerParams(vmem_limit_bytes=48 * 2**20),
        cost_estimate=pl.CostEstimate(flops=0, bytes_accessed=size, transcendentals=0),
    )(member.reshape(1), *inputs)


def slab_places(member, rows, step, slab):
    found = []
    for part, order in enumerate((TOPS, LOWS)):
        for turn in order:
            owner = member ^ turn
            for block in (2 * part, 2 * part + 1):
                found.append((owner, block * rows + owner * step))
    return found


def sort_heads_kernel(slots, rows, step, slab, member_ref, *refs):
    *got, out_ref, whole = refs
    member = member_ref[0]
    width = whole.shape[0]
    high = slots * HEAD
    for turn in range(4):
        owner = member ^ turn
        at = jnp.minimum(owner * high, width - high)
        spare = (owner * high - at) // HEAD
        if turn == 0:
            pass
        for slot in range(slots):

            @pl.when(slot >= spare)
            def _(turn=turn, slot=slot, at=at):
                to = pl.multiple_of(at + slot * HEAD, HEAD)
                whole[pl.ds(to, HEAD), :] = got[turn][slot * HEAD : (slot + 1) * HEAD, :]

    line = lax.broadcasted_iota(jnp.int32, (slab, 1), 0)
    for index, (owner, at) in enumerate(slab_places(member, rows, step, slab)):
        rows_here = whole[pl.ds(pl.multiple_of(at, 16), slab), :]
        keep = (line < step) | (owner == 3)
        out_ref[index * slab : (index + 1) * slab, :] = jnp.where(
            keep, rows_here, jnp.zeros_like(rows_here)
        )


def split_heads_kernel(slots, rows, step, slab, member_ref, value_ref, *refs):
    *outs, whole = refs
    member = member_ref[0]
    width = whole.shape[0]
    high = slots * HEAD
    for index, (owner, at) in enumerate(slab_places(member, rows, step, slab)):
        first = index * slab
        whole[pl.ds(pl.multiple_of(at, 16), step), :] = value_ref[first : first + step, :]

        @pl.when(owner == 3)
        def _(first=first, at=at):
            to = pl.multiple_of(at + step, 16)
            whole[pl.ds(to, slab - step), :] = value_ref[first + step : first + slab, :]

    for turn in range(4):
        owner = member ^ turn
        at = jnp.minimum(owner * high, width - high)
        spare = owner * high - at
        line = lax.broadcasted_iota(jnp.int32, (high, 1), 0)
        rows_here = whole[pl.ds(pl.multiple_of(at, HEAD), high), :]
        outs[turn][...] = jnp.where(line >= spare, rows_here, jnp.zeros_like(rows_here))


def member_rows(refs, member, owner, cut, rows):
    if member is None:
        at = owner * rows
        return [
            (ref[at : at + cut, :].astype(F32), ref[at + cut : at + rows, :].astype(F32))
            for ref in refs
        ]
    turn = member ^ owner
    twin = (turn & 1) * 2 + turn // 2
    found = []
    for ref in refs:
        top = ref[pl.ds(pl.multiple_of(twin * cut, 16), cut), :]
        low = ref[pl.ds(pl.multiple_of(4 * cut + turn * (rows - cut), 16), rows - cut), :]
        found.append((top.astype(F32), low.astype(F32)))
    return found


def blocks_into(out_ref, lines, value, block, padded):
    for index in range(value.shape[1] // padded):
        out_ref[lines, index * block : (index + 1) * block] = value[
            :, index * padded : index * padded + block
        ]


def finish_attn_kernel(slots, cut, total, _, left_ref, right_ref, out_ref):
    member = None
    rows = out_ref.shape[0]
    width = out_ref.shape[1] // 3
    high = slots * HEAD
    held = left_ref.shape[0] // 4
    for owner in range(4):
        start = min(owner * high, width - high)
        spare = owner * high - start
        (left, right) = member_rows((left_ref, right_ref), member, owner, cut, held)
        for lines, first, size in ((0, 0, cut), (1, cut, rows - cut)):
            shared = left[lines].shape[1] * 2 - total
            both = jnp.concatenate([left[lines], right[lines][:, shared:]], axis=1)
            for third in range(3):
                to = third * width + start + spare
                out_ref[first : first + size, to : to + high - spare] = both[
                    :size, third * high + spare : (third + 1) * high
                ]


def finish_proj_kernel(step, slab, cut, total, padded, member_ref, left_ref, right_ref, out_ref):
    member = member_ref[0]
    block = out_ref.shape[1] // 4
    for owner in range(4):
        size = slab if owner == 3 else step
        (left, right) = member_rows((left_ref, right_ref), member, owner, cut, slab)
        for lines, first, count in ((0, 0, cut), (1, cut, size - cut)):
            shared = left[lines].shape[1] * 2 - total
            both = jnp.concatenate([left[lines], right[lines][:, shared:]], axis=1)[:count]
            at = owner * step + first
            blocks_into(out_ref, slice(at, at + count), both, block, padded)


def finish_in_kernel(cut, padded, _, value_ref, out_ref):
    member = None
    rows = out_ref.shape[0]
    part = out_ref.shape[1] // 16
    for owner in range(4):
        ((top, low),) = member_rows((value_ref,), member, owner, cut, padded)
        for block in range(4):
            to = (block * 4 + owner) * part
            out_ref[:cut, to : to + part] = top[:, block * padded : block * padded + part]
            out_ref[cut:, to : to + part] = low[
                : rows - cut, block * padded : block * padded + part
            ]


def finish_out_kernel(cut, padded, _, value_ref, out_ref):
    member = None
    rows = out_ref.shape[0] // 4
    block = out_ref.shape[1] // 4
    for owner in range(4):
        ((top, low),) = member_rows((value_ref,), member, owner, cut, padded)
        at = owner * rows
        blocks_into(out_ref, slice(at, at + cut), top, block, padded)
        blocks_into(out_ref, slice(at + cut, at + rows), low[: rows - cut], block, padded)


def expand_kernel(padded, _, *refs):
    half = len(refs) // 2
    for value_ref, out_ref in zip(refs[:half], refs[half:]):
        block = value_ref.shape[1] // 4
        out_ref[...] = jnp.zeros_like(out_ref)
        for index in range(4):
            out_ref[:, index * padded : index * padded + block] = value_ref[
                :, index * block : (index + 1) * block
            ]


def edge_kernel(padded, section_ref, mine_ref, other_ref, edge_ref):
    block = edge_ref.shape[2] // 4
    wide = 4 * padded
    for side, refs in enumerate(((mine_ref, other_ref), (other_ref, mine_ref))):

        @pl.when(section_ref[0] == side)
        def _(side=side, refs=refs):
            for index, ref in enumerate(refs):
                value = ref[:, side * wide : (side + 1) * wide].astype(F32)
                blocks_into(edge_ref.at[index], slice(None), value, block, padded)


def order_kernel(forth, place_ref, value_ref, out_ref):
    n = value_ref.shape[0] // 8
    at = 0
    for part, order in enumerate((TOPS, LOWS)):
        for turn in order:
            rows = pl.ds(pl.multiple_of(((place_ref[0] ^ turn) * 2 + part) * n, n), n)
            if forth:
                out_ref[at : at + n, :] = value_ref[rows, :]
            else:
                out_ref[rows, :] = value_ref[at : at + n, :]
            at += n


def deal_kernel(whole_in, whole_out, places_ref, *refs):
    place = places_ref[0]
    count = 1 if whole_in else 4
    inputs, outs = refs[:count], refs[count:]
    size = inputs[0].shape[0] // (4 if whole_in else 1)
    for turn in range(4):
        at = pl.multiple_of((place ^ turn) * size, size)
        if whole_in:
            outs[turn][...] = inputs[0][pl.ds(at, size), :]
        elif whole_out:
            outs[0][pl.ds(at, size), :] = inputs[turn][...]
        else:
            for owner in range(4):

                @pl.when((place ^ turn) == owner)
                def _(turn=turn, owner=owner):
                    outs[turn][...] = inputs[owner][...]


def join_kernel(_, own, near_a, near_b, far_a, far_b, *out_refs):
    n, m = near_a.shape[0], near_b.shape[0]
    at = 0
    for part, first, size in (
        (own, 0, n),
        (near_a, 0, n),
        (far_a, 0, 2 * n),
        (own, n, m),
        (near_b, 0, m),
        (far_b, 0, 2 * m),
    ):
        column = 0
        for out_ref in out_refs:
            width = out_ref.shape[1]
            out_ref[at : at + size, :] = part[first : first + size, column : column + width]
            column += width
        at += size


def same_kernel(*refs):
    pass


def tie(value, *others):
    any_place = pl.BlockSpec(memory_space=pl.ANY)
    return pl.pallas_call(
        same_kernel,
        in_specs=[any_place] * (1 + len(others)),
        out_specs=any_place,
        out_shape=jax.ShapeDtypeStruct(value.shape, value.dtype),
        input_output_aliases={0: 0},
        cost_estimate=pl.CostEstimate(flops=0, bytes_accessed=0, transcendentals=0),
    )(value, *others)


def body(
    replicas,
    shards,
    boundary,
    segments,
    attn_weight,
    proj_weight,
    fc_in_weight,
    fc_out_weight,
    norm_gains,
    vector_bias,
    fc_in_bias,
):
    sub = shards // replicas
    team = replicas * sub
    fast = replicas == 4 and sub == 1
    team_axes = ("replica", "sub")
    row_axes = ("seq", "sub")
    chip_axes = ("replica", "seq", "sub")
    section = lax.axis_index("section")
    first = section == 0
    member = lax.axis_index(team_axes)
    local = boundary.shape[3]
    width = boundary.shape[4]
    hidden = fc_in_bias.shape[1]
    n = local // 2
    length = segments.shape[2]
    half = length // 2
    slots = -(-HEADS // team)
    heads_width = slots * HEAD
    hid = hidden // team
    block = width // 4
    padded = -(-block // 32) * 32 if fast else block
    wide = 4 * padded
    mask = None
    if fast:
        mask = (jnp.arange(wide) % padded < block).astype(F32)
    mixed_rows = -(-3 * heads_width // 128) * 128 if fast else 3 * heads_width
    attn_half = -(-mixed_rows // 256) * 128
    proj_half = -(-wide // 256) * 128

    def head_start(index):
        return jnp.minimum(index * slots, HEADS - slots)

    def spare_heads(index):
        return min(max(index * slots - (HEADS - slots), 0), slots)

    start = head_start(member) * HEAD

    def cross(value, pairs=SWAP):
        return lax.ppermute(value, "section", pairs)

    def side(value):
        return lax.ppermute(value, "replica", SIDE)

    def across(value):
        return lax.ppermute(value, "replica", ACROSS)

    def corner(value):
        return lax.ppermute(value, "replica", CORNER)

    def pick(a, b):
        return jnp.where(first, a, b)

    def halves(value, half, axis):
        size = value.shape[axis]
        left = lax.slice_in_dim(value, 0, half, axis=axis)
        right = lax.slice_in_dim(value, size - half, size, axis=axis)
        return pick(left, right), pick(right, left)

    def spaced(vector):
        if not fast:
            return vector
        parts = vector.reshape(-1, 4, block)
        parts = jnp.pad(parts, ((0, 0), (0, 0), (0, padded - block)))
        return parts.reshape(vector.shape[:-1] + (wide,))

    def dense(vector):
        if not fast:
            return vector
        return vector.reshape(vector.shape[:-1] + (4, padded))[..., :block].reshape(
            vector.shape[:-1] + (width,)
        )

    def flat(p, z):
        return p * shards + z

    rounds = []
    for turn in range(2):
        pairs = []
        for p in range(replicas):
            for z in range(shards):
                slot = z // (shards // 2)
                h = turn if slot == 0 else 1 - turn
                j = 2 * (z % (shards // 2)) + h
                target = flat(j // sub, p * sub + j % sub)
                pairs.append((flat(p, z), target))
        rounds.append(pairs)
    place = lax.axis_index(row_axes)
    early = place < shards // 2
    even = member % 2 == 0

    def to_team_far(value):
        top, low = value[:n], value[n:]
        one = lax.ppermute(jnp.where(early, top, low), chip_axes, rounds[0])
        two = lax.ppermute(jnp.where(early, low, top), chip_axes, rounds[1])
        return jnp.concatenate([jnp.where(even, one, two), jnp.where(even, two, one)])

    def from_team_far(value):
        top, low = value[:n], value[n:]
        one = lax.ppermute(
            jnp.where(even, top, low), chip_axes, [(b, a) for a, b in rounds[0]]
        )
        two = lax.ppermute(
            jnp.where(even, low, top), chip_axes, [(b, a) for a, b in rounds[1]]
        )
        return jnp.concatenate([jnp.where(early, one, two), jnp.where(early, two, one)])

    plane = lax.axis_index("seq")

    def turned(pieces, axis):
        own, *others = pieces
        return [own] + [
            lax.ppermute(x, axis, pairs) for x, pairs in zip(others, (SIDE, ACROSS, CORNER))
        ]

    def dealt(place, pieces, whole_in, whole_out):
        rows, columns = pieces[0].shape
        if whole_in:
            outs = [jax.ShapeDtypeStruct((rows // 4, columns), BF)] * 4
        elif whole_out:
            outs = [jax.ShapeDtypeStruct((rows * 4, columns), BF)]
        else:
            outs = [jax.ShapeDtypeStruct((rows, columns), BF)] * 4
        return kernel_call(partial(deal_kernel, whole_in, whole_out), place, pieces, outs)

    def to_team(value):
        if not fast:
            return to_team_far(value)
        pieces = turned(dealt(member, [value], True, False), "replica")
        pieces = turned(dealt(plane ^ member, pieces, False, False), "seq")
        return dealt(plane, pieces, False, True)[0]

    def from_team(value):
        if not fast:
            return from_team_far(value)
        pieces = turned(dealt(plane, [value], True, False), "seq")
        pieces = turned(dealt(plane ^ member, pieces, False, False), "replica")
        return dealt(member, pieces, False, True)[0]

    if fast:
        order_a = [member, member ^ 2, member ^ 1, member ^ 3]
        order_b = [member, member ^ 1, member ^ 2, member ^ 3]
    else:
        order_a = order_b = list(range(team))

    def gather_near(value, cut, widths=None):
        a, b = value[:cut], value[cut:]
        if not fast:
            whole = jnp.concatenate(
                [
                    lax.all_gather(a, team_axes, axis=0, tiled=True),
                    lax.all_gather(b, team_axes, axis=0, tiled=True),
                ]
            )
            return whole, whole
        near_a, near_b = across(a), side(b)
        return gather_far(value, cut, near_a, near_b, widths), near_b

    def gather_far(value, cut, near_a, near_b, widths=None):
        a, b = value[:cut], value[cut:]
        far_a = side(jnp.concatenate([a, near_a]))
        far_b = across(jnp.concatenate([b, near_b]))
        outs = [
            jax.ShapeDtypeStruct((4 * value.shape[0], width), value.dtype)
            for width in widths or [value.shape[1]]
        ]
        parts = [value, near_a, near_b, far_a, far_b]
        outs = kernel_call(join_kernel, member, parts, outs)
        return outs if widths else outs[0]

    def gather(value, cut):
        return gather_near(value, cut)[0]

    def gather_many(values, cut):
        whole = jnp.concatenate(values, axis=1)
        return gather_near(whole, cut, [value.shape[1] for value in values])[0]

    def ordered(forth, value):
        out = jax.ShapeDtypeStruct(value.shape, value.dtype)
        return kernel_call(partial(order_kernel, forth), member, [value], [out])[0]

    def gather_late(value):
        if not fast:
            return gather(value, n)
        whole = lax.all_gather(value, "replica", axis=0, tiled=True)
        return ordered(True, whole)

    def scatter_late(value):
        if not fast:
            return scatter(value)
        whole = ordered(False, value)
        return lax.psum_scatter(whole, "replica", scatter_dimension=0, tiled=True)


    def scatter(value, got=None):
        middle_row = value.shape[0] // 2
        a, b = value[:middle_row], value[middle_row:]
        if not fast:
            return jnp.concatenate(
                [
                    lax.psum_scatter(a.astype(F32), team_axes, scatter_dimension=0, tiled=True),
                    lax.psum_scatter(b.astype(F32), team_axes, scatter_dimension=0, tiled=True),
                ]
            )
        m = middle_row // 4
        got_a, got_b = got or scatter_first(value)
        sent_a = (a[m : 2 * m].astype(F32) + got_a[m:]).astype(BF)
        sent_b = (b[m : 2 * m].astype(F32) + got_b[m:]).astype(BF)
        last_a, last_b = across(sent_a), side(sent_b)
        sum_a = a[:m].astype(F32) + got_a[:m] + last_a
        sum_b = b[:m].astype(F32) + got_b[:m] + last_b
        return jnp.concatenate([sum_a, sum_b])

    def scatter_first(value):
        middle_row = value.shape[0] // 2
        m = middle_row // 4
        return side(value[2 * m : middle_row]), across(value[middle_row + 2 * m :])

    if fast:
        rows = width // replicas
        slab = -(-rows // 64) * 16
        step = (rows - slab) // 3
        cut = padded // 2
        sorted_heads = jax.ShapeDtypeStruct((16 * slab, 2 * n), BF)
        one = jax.ShapeDtypeStruct((heads_width, 2 * n), BF)
        scratch = [pltpu.VMEM((width, 2 * n), BF)]

    def heads_to_tokens(values):
        if fast:
            own, near, over, far = values
            got = [own, side(near), across(over), corner(far)]
            kernel = partial(sort_heads_kernel, slots, rows, step, slab)
            return kernel_call(kernel, member, got, [sorted_heads], scratch)[0]
        pieces = values[0].reshape(heads_width, 2, team, n).transpose(2, 0, 1, 3)
        got = lax.all_to_all(pieces, team_axes, 0, 0, tiled=True)
        got = got.reshape(team, heads_width, 2 * n)
        pieces = []
        for index in range(team):
            spare = spare_heads(index) * HEAD
            if spare < heads_width:
                pieces.append(got[index, spare:])
        return jnp.concatenate(pieces)

    def tokens_to_heads(value):
        if fast:
            kernel = partial(split_heads_kernel, slots, rows, step, slab)
            own, near, over, far = kernel_call(kernel, member, [value], [one] * 4, scratch)
            return [own, side(near), across(over), corner(far)]

        def of(index):
            return lax.dynamic_slice_in_dim(value, head_start(index) * HEAD, heads_width, 0)

        pieces = jnp.stack([of(index) for index in range(team)])
        got = lax.all_to_all(pieces, team_axes, 0, 0, tiled=True)
        got = got.reshape(team, heads_width, 2, n).transpose(1, 2, 0, 3)
        whole = got.reshape(heads_width, length)
        spare = member * slots - head_start(member)
        lines = lax.broadcasted_iota(jnp.int32, (heads_width, 1), 0)
        return [jnp.where(lines >= spare * HEAD, whole, jnp.zeros_like(whole))]

    def head_columns(weight):
        return [
            lax.dynamic_slice_in_dim(weight, third * width + start, heads_width, 1)
            for third in range(3)
        ]

    if fast:
        hid_part = hid // replicas
        more = padded - rows
        own_attn = jnp.concatenate(head_columns(attn_weight[0]), axis=1)
        own_attn = jnp.pad(own_attn, ((0, more), (0, mixed_rows - 3 * heads_width)))
        own_in = jnp.concatenate(
            [
                jnp.pad(
                    lax.dynamic_slice_in_dim(
                        fc_in_weight[0], part * hid + member * hid_part, hid_part, 1
                    ),
                    ((0, more), (0, padded - hid_part)),
                )
                for part in range(replicas)
            ],
            axis=1,
        )
        own_out = lax.dynamic_slice_in_dim(fc_out_weight[0], member * hid_part, hid_part, 0)
        own_proj = lax.dynamic_slice_in_dim(proj_weight[0], member * step, slab, 0)
        own_out, own_proj = kernel_call(
            partial(expand_kernel, padded),
            member,
            [own_out, own_proj],
            [jax.ShapeDtypeStruct((hid_part, wide), BF), jax.ShapeDtypeStruct((slab, wide), BF)],
        )
        own_out = jnp.pad(own_out, ((0, padded - hid_part), (0, 0)))

        def gathered(piece):
            return lax.all_gather(piece, "seq", axis=0, tiled=True)

        def full(mine):
            other = cross(mine)
            return pick(mine, other), pick(other, mine)

        def spread(pair):
            got = cross(pair[1])
            return pick(pair[0], got), pick(got, pair[0])

        attn_pieces = spread(halves(own_attn, attn_half, 1))
        fc_pieces = spread((pick(own_in, own_out), pick(own_out, own_in)))
        shared = 2 * attn_half - mixed_rows
        attn_got = [gathered(attn_pieces[0])]
        proj_got = []
        fc_got = []
        proj_whole = []

        def fetch_proj(after):
            proj_got.append(gathered(tie(own_proj, after)))

        def fetch_fc(layer, after):
            fc_got.append(gathered(tie(fc_pieces[layer], after)))

        def fetch_attn(after):
            attn_got.append(gathered(tie(attn_pieces[1], after)))

        def get_attn(layer, after):
            left, right = full(tie(attn_got[layer], after))
            return jnp.concatenate([left, right[:, shared:]], axis=1)

        def get_proj(layer, near=None, after=None):
            if layer == 0:
                mine = tie(proj_got[0], near)
                near = across(mine[: 2 * slab]), side(mine[2 * slab :])
                near = [tie(value, after) for value in near]
                mine = gather_far(mine, 2 * slab, *near)
                other = cross(mine)
                proj_whole.extend([pick(mine, other), pick(other, mine)])
            return proj_whole[layer]

        def get_fc(layer, after):
            return full(tie(fc_got[layer], after))

        def hid_of(vector):
            mine = lax.dynamic_slice_in_dim(
                vector.reshape(replicas, replicas, hid_part), member, 1, 1
            )
            return jnp.pad(mine[:, 0], ((0, 0), (0, padded - hid_part))).reshape(wide)

        def hid_into(vector):
            zeros = jnp.zeros((replicas, replicas, hid_part), F32)
            return lax.dynamic_update_slice_in_dim(
                zeros, vector.reshape(replicas, 1, padded)[..., :hid_part], member, 1
            ).reshape(hidden)

    else:

        def both(value):
            other = cross(value)
            return pick(value, other), pick(other, value)

        def weights_of(layer):
            def whole(weight):
                return lax.all_gather(both(weight[0])[layer], row_axes, axis=0, tiled=True)

            w_attn = jnp.concatenate(head_columns(whole(attn_weight)), axis=1)
            w_proj = whole(proj_weight)
            w_in = lax.dynamic_slice_in_dim(whole(fc_in_weight), member * hid, hid, 1)
            w_out = lax.dynamic_slice_in_dim(whole(fc_out_weight), member * hid, hid, 0)
            return w_attn, w_proj, w_in, w_out

        whole_weights = [weights_of(0), weights_of(1)]

        def fetch_proj(after):
            pass

        def fetch_fc(layer, after):
            pass

        fetch_attn = fetch_proj

        def get_attn(layer, after):
            return whole_weights[layer][0]

        def get_proj(layer, *others):
            return whole_weights[layer][1]

        def get_fc(layer, after):
            return whole_weights[layer][2:]

        def hid_of(vector):
            return lax.dynamic_slice_in_dim(vector, member * hid, hid, 0)

        def hid_into(vector):
            return lax.dynamic_update_slice_in_dim(
                jnp.zeros((hidden,), F32), vector, member * hid, 0
            )

    def heads_into(vector):
        return lax.dynamic_update_slice_in_dim(jnp.zeros((width,), F32), vector, start, 0)

    block_0, block_1 = boundary[0, 0, 0], boundary[0, 1, 0]
    if fast:
        block_0, block_1 = kernel_call(
            partial(expand_kernel, padded),
            member,
            [block_0, block_1],
            [jax.ShapeDtypeStruct((local, wide), BF)] * 2,
        )
    kept = pick(block_0, block_1)
    got = cross(pick(block_1, block_0))
    source = to_team(pick(kept, got))
    cotangent = pick(got, kept)
    vectors = jnp.concatenate([norm_gains[0].ravel(), vector_bias[0].ravel(), fc_in_bias[0]])
    other_vectors = cross(vectors)
    vectors = (pick(vectors, other_vectors), pick(other_vectors, vectors))

    ids = lax.dynamic_index_in_dim(segments, section, 0, keepdims=False)[0]
    swapped = [
        (flat(p, z * sub + k), flat(z, p * sub + k))
        for p in range(replicas)
        for z in range(replicas)
        for k in range(sub)
    ]
    ids = lax.ppermute(ids, chip_axes, swapped).reshape(2, team, n)
    places, names = [], []
    for chunk, order in enumerate((order_a, order_b)):
        for index in order:
            places.append(chunk * half + index * n + jnp.arange(n, dtype=jnp.int32))
            names.append(lax.dynamic_index_in_dim(ids[chunk], index, 0, keepdims=False))
    if fast:
        places, names = [], []
        ids = ids.reshape(2, 2, team, n // 2)
        for chunk, order in enumerate((order_a, order_b)):
            for index in order:
                for part in range(2):
                    at = chunk * half + part * (half // 2) + index * (n // 2)
                    places.append(at + jnp.arange(n // 2, dtype=jnp.int32))
                    names.append(
                        lax.dynamic_index_in_dim(ids[chunk, part], index, 0, keepdims=False)
                    )
    places, names = jnp.concatenate(places), jnp.concatenate(names)
    allowed = (names[:, None] == names[None, :]) & (places[:, None] <= places[None, :])
    bias = jnp.where(allowed, 0.0, MASKED).astype(F32)

    def parameters(layer):
        vector = vectors[layer]
        lines = vector[: 8 * width].reshape(8, width)
        query_bias = lax.dynamic_slice_in_dim(lines[3], start, heads_width, 0)
        value_bias = lax.dynamic_slice_in_dim(lines[4], start, heads_width, 0)
        lines = spaced(lines)
        gains, biases = lines[:2], lines[2:]
        hid_bias = hid_of(vector[8 * width :])
        mixed_bias = jnp.concatenate([query_bias, jnp.zeros_like(query_bias), value_bias])
        mixed_bias = jnp.pad(mixed_bias, (0, mixed_rows - mixed_bias.shape[0]))
        return gains, biases, hid_bias, mixed_bias

    def enter(layer, value):
        gains, biases, _, _ = parameters(layer)
        normed = (norm_stats(value, mask, width)[0] * gains[0] + biases[0]).astype(BF)
        return gather_near(normed, n)

    def mix(layer, normed, w_attn, *others):
        mixed_bias = parameters(layer)[3]
        if fast and others:
            mixed_bias = tie(mixed_bias, *others)
        return (dot(w_attn, normed, (0, 1)) + mixed_bias[:, None]).astype(BF)

    def forward(layer, value, normed, mixed, w_proj, hold):
        gains, biases, hid_bias, _ = parameters(layer)
        proj_bias = tie(biases[3], fc_got[0]) if fast and layer == 0 else biases[3]
        attended, lse = attend(mixed, bias, slots, fast)
        if layer == 0:
            w_proj.append(get_proj(0, near, lse))
        w_proj = w_proj[layer]
        attended = heads_to_tokens(attended)
        middle = value + dot(attended, w_proj, (0, 0)) + proj_bias
        gain = hold(gains[1])
        normed_two = (norm_stats(middle, mask, width)[0] * gain + biases[4]).astype(BF)
        w_in, w_out = get_fc(layer, normed_two)
        normed_two = gather(normed_two, n)
        activated, slope = gelu_pair(dot(normed_two, w_in, (1, 0)) + hid_bias)
        activated, slope = lax.optimization_barrier((activated.astype(BF), slope.astype(BF)))
        kept = (value, normed, mixed, lse, attended, middle, normed_two, activated, slope)
        return kept, (w_in, w_out)

    def leave(layer, middle, activated, w_out):
        return dot(activated, w_out, (1, 0)).astype(BF)

    ones = lax.optimization_barrier(jnp.ones((16, length), BF))

    def backward(layer, grad_out, grad_low, kept, weights, fillers):
        value, normed, mixed, lse, attended, middle, normed_two, activated, slope = kept
        w_attn, w_proj, w_in, w_out = weights
        gains = parameters(layer)[0]
        low_sum = jnp.sum(grad_out, axis=0)
        grad_pre = (dot(grad_low, w_out, (1, 1)) * slope).astype(BF)
        part = dot(grad_pre, w_in, (1, 1)).astype(BF)
        fillers[0](part)
        grad_two = scatter(part)
        if fast:
            sent = dot(pick(activated, normed_two), pick(grad_low, grad_pre), (0, 0))
            sent = cross(sent.astype(BF))
            fc_pair = (pick(normed_two, activated), pick(grad_pre, grad_low), sent)
        else:
            fc_pair = (
                dot(normed_two, grad_pre, (0, 0)).astype(BF),
                dot(activated, grad_low, (0, 0)).astype(BF),
            )
        fillers[1](part)
        hid_sum = dot(ones, grad_pre, (1, 0))[0]
        gain = fillers[4](gains[1])
        grad_norm, gain_two, shift_two = norm_back(grad_two, middle, gain, mask, width)
        grad_middle = grad_out + grad_norm
        grad_branch = grad_middle.astype(BF)
        branch_sum = jnp.sum(grad_branch.astype(F32), axis=0)
        grad_attended = dot(w_proj, grad_branch, (1, 1)).astype(BF)
        grad_attended = tokens_to_heads(grad_attended)
        own, other = halves(grad_branch, proj_half, 1)
        if fast:
            sent = cross(dot(attended, other, (1, 0)).astype(BF))
            fc_total = (dot(fc_pair[0], fc_pair[1], (0, 0)) + fc_pair[2]).astype(BF)
            proj_total = (dot(attended, own, (1, 0)) + sent).astype(BF)
        else:
            fc_total = fc_pair
            proj_total = dot(attended, grad_branch, (1, 0)).astype(BF)
        fillers[2](grad_attended[-1], fc_total, proj_total)
        lse = fillers[3](lse, proj_total)
        grad_mixed = attend_back(mixed, grad_attended, bias, lse, slots, fast)
        part = dot(grad_mixed, w_attn, (0, 1)).astype(BF)
        grad_one = scatter(part)
        own, other = halves(grad_mixed, attn_half, 0)
        if fast:
            attn_pair = (own, cross(dot(normed, other, (0, 1)).astype(BF)))
            attn_total = (dot(normed, attn_pair[0], (0, 1)) + attn_pair[1]).astype(BF)
        else:
            attn_total = dot(normed, grad_mixed, (0, 1)).astype(BF)
        mixed_sum = jnp.sum(grad_mixed.astype(F32), axis=1)
        gain = fillers[5](gains[0])
        grad_norm, gain_one, shift_one = norm_back(grad_one, value, gain, mask, width)
        grad_in = grad_middle + grad_norm
        query_sum = heads_into(mixed_sum[:heads_width])
        value_sum = heads_into(mixed_sum[2 * heads_width : 3 * heads_width])
        lines = dense(
            jnp.stack([gain_one, gain_two, shift_one, branch_sum, shift_two, low_sum])
        )
        small = jnp.concatenate(
            [
                lines[:3].ravel(),
                query_sum,
                value_sum,
                lines[3:].ravel(),
                hid_into(hid_sum),
            ]
        )
        return grad_in, small, fc_total, proj_total, attn_total, grad_mixed

    if fast:

        proj_cut = (slab // 32) * 16

        def over_planes(total):
            return lax.psum_scatter(total, "seq", scatter_dimension=0, tiled=True)

        def both(mine_0, mine_1):
            return (mine_0, cross(mine_0, [(1, 0)])), (mine_1, cross(mine_1, [(0, 1)]))

        def finish(kernel, pairs, shape):
            (mine_0, other_0), (mine_1, other_1) = pairs
            left, right = pick(mine_0, other_1), pick(other_0, mine_1)
            out = jax.ShapeDtypeStruct(shape, F32)
            return kernel_call(kernel, member, [left, right], [out])[0]

        def finish_fc(pairs):
            (mine_0, other_0), (mine_1, other_1) = pairs
            left, right = pick(mine_0, other_1), pick(other_0, mine_1)
            w_in = kernel_call(
                partial(finish_in_kernel, cut, padded),
                member,
                [left],
                [jax.ShapeDtypeStruct((rows, hidden), F32)],
            )[0]
            w_out = kernel_call(
                partial(finish_out_kernel, cut, padded),
                member,
                [right],
                [jax.ShapeDtypeStruct((hid, width), F32)],
            )[0]
            return w_in, w_out

        def reduce_small(small):
            total = pick(small[0], small[1]) + cross(pick(small[1], small[0]))
            total = total.reshape(-1, 128)
            for axis, pairs in (
                ("replica", SIDE),
                ("replica", ACROSS),
                ("seq", SIDE),
                ("seq", CORNER),
            ):
                total = total + lax.ppermute(total, axis, pairs)
            return total.reshape(-1)

    held = {}

    def nothing(*_):
        pass

    def same(value, *_):
        return value

    values = source.astype(F32)
    fetch_proj(source)
    normed, near = enter(0, values)
    fetch_fc(0, near)
    attn_weights = [get_attn(0, source)]
    cotangent = to_team(cotangent)
    mixed = mix(0, normed, attn_weights[0], cotangent)
    proj_weights = []
    fetch_attn(mixed)
    fetch_fc(1, mixed)
    kept_0, fc_0 = forward(0, values, normed, mixed, proj_weights, same)
    part = leave(0, kept_0[5], kept_0[7], fc_0[1])
    attn_weights.append(get_attn(1, part))
    passed = kept_0[5] + scatter(part) + parameters(0)[1][5]
    values = passed.astype(BF).astype(F32)
    normed, near = enter(1, values)
    mixed = mix(1, normed, attn_weights[1])
    proj_weights.append(get_proj(1))
    grad_low = gather_late(cotangent)

    def hold_low(value):
        return tie(value, grad_low) if fast else value

    kept_1, fc_1 = forward(1, values, normed, mixed, proj_weights, hold_low)
    weights_0 = (attn_weights[0], proj_weights[0], *fc_0)
    weights_1 = (attn_weights[1], proj_weights[1], *fc_1)

    def finish_forward(part):
        held["out"] = scatter_late(leave(1, kept_1[5], kept_1[7], fc_1[1]))

    def start_fc(layer):
        def start(grad_attended, fc_total, proj_total):
            if fast:
                held[layer] = over_planes(fc_total)

        return start

    fillers = (nothing, finish_forward, start_fc(1), same, same, same)
    grad, small_1, fc_1, proj_1, attn_1, _ = backward(
        1, cotangent.astype(F32), grad_low, kept_1, weights_1, fillers
    )
    out = (kept_1[5] + held["out"] + parameters(1)[1][5]).astype(BF)
    grad = grad.astype(BF)
    grad_low = gather(grad, n)
    fillers = (nothing, nothing, start_fc(0), same, same, same)
    if fast:
        attn_1 = over_planes(attn_1)

        held["fc_1"] = lax.all_gather(held[1], "replica", axis=0, tiled=True)

        held["attn_1"] = lax.all_gather(attn_1, "replica", axis=0, tiled=True)

        def hold_sums(value, proj_0):
            held["proj"] = whole = jnp.concatenate([proj_0, proj_1], axis=1)
            held["got"] = scatter_first(whole)
            return tie(value, *held["got"])

        def hold_attn(value):
            return tie(value, held["attn_1"])

        def hold_gathered(value):
            return tie(value, held["fc_1"])

        fillers = (nothing, nothing, start_fc(0), hold_sums, hold_gathered, hold_attn)
    grad, small_0, fc_0, proj_0, attn_0, grad_mixed = backward(
        0, grad.astype(F32), grad_low, kept_0, weights_0, fillers
    )
    grad = grad.astype(BF)
    if fast:
        proj = scatter(held["proj"], held["got"]).astype(BF)
        proj = over_planes(proj)
        attn_0 = over_planes(attn_0)
        mine = from_team(jnp.concatenate([grad, out], axis=1))
        edge = kernel_call(
            partial(edge_kernel, padded),
            section,
            [mine, cross(mine)],
            [jax.ShapeDtypeStruct((2, local, width), F32)],
        )[0]
        fc_0 = ordered(False, gather(tie(held[0], grad), cut))
        fc = both(fc_0, held["fc_1"])
        attn = both(ordered(False, gather(attn_0, cut)), held["attn_1"])
        proj = both(*gather_many([proj[:, :proj_half], proj[:, proj_half:]], proj_cut))
    else:
        out, grad = from_team(out), from_team(grad)
        got_out, got_grad = cross(out, [(0, 1)]), cross(grad, [(1, 0)])
        edge = jnp.stack([pick(grad, got_out), pick(got_grad, out)]).astype(F32)
    edge = edge.reshape(1, 2, 1, local, width)
    if fast:
        in_sum, out_sum = finish_fc(fc)
        kernel = partial(finish_proj_kernel, step, slab, proj_cut, wide, padded)
        proj_sum = finish(kernel, proj, (rows, width))
        kernel = partial(finish_attn_kernel, slots, cut, mixed_rows)
        attn_sum = finish(kernel, attn, (rows, 3 * width))
        small = reduce_small((small_0, small_1))
    else:

        def summed(make, after):
            parts = [lax.optimization_barrier((make(layer), after))[0] for layer in range(2)]
            mine = pick(parts[0], parts[1]) + cross(pick(parts[1], parts[0]))
            mine = lax.psum_scatter(mine, row_axes, scatter_dimension=0, tiled=True)
            return lax.psum(mine.astype(F32), ("replica",))

        def attn_whole(layer):
            value = (attn_0, attn_1)[layer]
            zeros = jnp.zeros((width, width), BF)
            parts = [value[:, i * heads_width : (i + 1) * heads_width] for i in range(3)]
            return jnp.concatenate(
                [lax.dynamic_update_slice_in_dim(zeros, x, start, 1) for x in parts], axis=1
            )

        def proj_whole(layer):
            return (proj_0, proj_1)[layer]

        def in_whole(layer):
            zeros = jnp.zeros((width, hidden), BF)
            part = (fc_0, fc_1)[layer][0]
            return lax.dynamic_update_slice_in_dim(zeros, part, member * hid, 1)

        def out_whole(layer):
            zeros = jnp.zeros((hidden, width), BF)
            part = (fc_0, fc_1)[layer][1]
            return lax.dynamic_update_slice_in_dim(zeros, part, member * hid, 0)

        attn_sum = summed(attn_whole, edge)
        proj_sum = summed(proj_whole, attn_sum)
        in_sum = summed(in_whole, proj_sum)
        out_sum = summed(out_whole, in_sum)
        small = pick(small_0, small_1) + cross(pick(small_1, small_0))
        small = lax.psum(small, chip_axes)
    return (
        edge,
        attn_sum[None],
        proj_sum[None],
        in_sum[None],
        out_sum[None],
        small[: 2 * width].reshape(1, 2, width),
        small[2 * width : 8 * width].reshape(1, 6, width),
        small[8 * width :][None],
    )


def solution(mesh):
    sections, replicas, shards = (mesh.shape[name] for name in ("section", "replica", "shard"))
    split = Mesh(
        mesh.devices.reshape(sections, replicas, replicas, shards // replicas),
        ("section", "replica", "seq", "sub"),
    )
    rows = ("seq", "sub")
    return jax.shard_map(
        partial(body, replicas, shards),
        mesh=split,
        in_specs=(
            P("section", None, "replica", rows, None),
            P(None, "replica", None),
            P("section", rows, None),
            P("section", rows, None),
            P("section", rows, None),
            P("section", rows, None),
            P("section", None, None),
            P("section", None, None),
            P("section", None),
        ),
        out_specs=(
            P("section", None, "replica", rows, None),
            P("section", rows, None),
            P("section", rows, None),
            P("section", rows, None),
            P("section", rows, None),
            P("section", None, None),
            P("section", None, None),
            P("section", None),
        ),
        check_vma=False,
    )
```

```python
from functools import partial

import jax
import jax.numpy as jnp
from jax import lax
from jax.experimental import pallas as pl
from jax.experimental.pallas import tpu as pltpu
from jax.sharding import Mesh, PartitionSpec as P

HEADS = 25
HEAD = 64
EPSILON = 1e-05
MASKED = -1e30
BF = jnp.bfloat16
F32 = jnp.float32
SWAP = [(0, 1), (1, 0)]
SIDE = [(0, 1), (1, 0), (2, 3), (3, 2)]
ACROSS = [(0, 2), (2, 0), (1, 3), (3, 1)]
CORNER = [(0, 3), (3, 0), (1, 2), (2, 1)]


def dot(left, right, contract):
    return lax.dot_general(
        left, right, ((contract[:1], contract[1:]), ((), ())), preferred_element_type=F32
    )


def norm_stats(value, mask, width):
    mean = jnp.sum(value, axis=-1, keepdims=True) * (1.0 / width)
    centred = value - mean if mask is None else (value - mean) * mask
    variance = jnp.sum(centred * centred, axis=-1, keepdims=True) * (1.0 / width)
    inverse = lax.rsqrt(variance + EPSILON)
    return centred * inverse, inverse


def norm_back(grad, value, gain, mask, width):
    unit, inverse = norm_stats(value, mask, width)
    grad_unit = grad * gain
    mean_one = jnp.sum(grad_unit, axis=-1, keepdims=True) * (1.0 / width)
    mean_two = jnp.sum(grad_unit * unit, axis=-1, keepdims=True) * (1.0 / width)
    grad_value = inverse * (grad_unit - mean_one - unit * mean_two)
    if mask is not None:
        grad_value = grad_value * mask
    return grad_value, jnp.sum(grad * unit, axis=0), jnp.sum(grad, axis=0)


def gelu_pair(x):
    c = 0.7978845608028654
    square = x * x
    th = jnp.tanh(c * x * (1.0 + 0.044715 * square))
    value = 0.5 * x * (1.0 + th)
    slope = 0.5 * (1.0 + th) + 0.5 * x * (1.0 - th * th) * c * (1.0 + 3 * 0.044715 * square)
    return value, slope


def spots(chunk, piece, block, n, teams):
    order = ((0, 2, 1, 3), (0, 1, 2, 3))[chunk]
    return [
        (index * n, order[piece * (block // n) + index], chunk * n) for index in range(block // n)
    ]


def attend_kernel(grouped, q_ref, k_ref, v_ref, bias_ref, *out_refs):
    *outs, lse_ref = out_refs
    length = q_ref.shape[1]
    half = length // 2
    n = half // 4
    block = min(256, half)
    for chunk in range(2):
        extent = half * (chunk + 1)
        for piece in range(half // block):
            at = chunk * half + piece * block
            query = q_ref[:, at : at + block] * jnp.asarray(HEAD ** (-0.5), BF)
            scores = dot(k_ref[:, :extent], query, (0, 0)) + bias_ref[:extent, at : at + block]
            best = jnp.max(scores, axis=0, keepdims=True)
            weights = jnp.exp(scores - best)
            total = jnp.sum(weights, axis=0, keepdims=True)
            out = dot(v_ref[:, :extent], weights.astype(BF), (1, 0)) / total
            out = out.astype(BF)
            if grouped:
                for here, owner, there in spots(chunk, piece, block, n, 4):
                    outs[owner][:, there : there + n] = out[:, here : here + n]
            else:
                outs[0][:, at : at + block] = out
            lse_ref[0, :, at : at + block] = best + jnp.log(total)


def attend_back_kernel(grouped, q_ref, k_ref, v_ref, bias_ref, lse_ref, *refs):
    *g_refs, out_ref, keys, values = refs
    head = pl.program_id(0)
    slots = pl.num_programs(0)
    length = q_ref.shape[1]
    half = length // 2
    n = half // 4
    block = min(256, half)
    scale = HEAD ** (-0.5)
    keys[...] = jnp.zeros_like(keys)
    values[...] = jnp.zeros_like(values)
    for chunk in range(2):
        extent = half * (chunk + 1)
        for piece in range(half // block):
            at = chunk * half + piece * block
            query = q_ref[:, at : at + block] * jnp.asarray(scale, BF)
            if grouped:
                grad = jnp.concatenate(
                    [
                        g_refs[owner][:, there : there + n]
                        for _, owner, there in spots(chunk, piece, block, n, 4)
                    ],
                    axis=1,
                )
            else:
                grad = g_refs[0][:, at : at + block]
            scores = dot(k_ref[:, :extent], query, (0, 0)) + bias_ref[:extent, at : at + block]
            probs = jnp.exp(scores - lse_ref[0, :, at : at + block])
            inner = dot(v_ref[:, :extent], grad, (0, 0))
            rowdot = jnp.sum(probs * inner, axis=0, keepdims=True)
            dscore = (probs * (inner - rowdot)).astype(BF)
            values[:, :extent] += dot(grad, probs.astype(BF), (1, 1))
            keys[:, :extent] += dot(query, dscore, (1, 1))
            grad_query = (dot(k_ref[:, :extent], dscore, (1, 0)) * scale).astype(BF)
            out_ref[pl.ds(pl.multiple_of(head * HEAD, HEAD), HEAD), at : at + block] = grad_query
    key_rows = pl.ds(pl.multiple_of((slots + head) * HEAD, HEAD), HEAD)
    value_rows = pl.ds(pl.multiple_of((2 * slots + head) * HEAD, HEAD), HEAD)
    out_ref[key_rows, :] = keys[...].astype(BF)
    out_ref[value_rows, :] = values[...].astype(BF)

    @pl.when(head == 0)
    def _():
        used = 3 * HEAD * pl.num_programs(0)
        spare = out_ref.shape[0] % (3 * HEAD)
        if spare:
            rest = pl.ds(pl.multiple_of(used, HEAD), spare)
            out_ref[rest, :] = jnp.zeros((spare, length), BF)


def attend(mixed, bias, slots, grouped):
    length = mixed.shape[1]
    part = lambda first: pl.BlockSpec((HEAD, length), lambda h: (first + h, 0))
    whole = pl.BlockSpec((length, length), lambda h: (0, 0))
    count, span = (4, length // 4) if grouped else (1, length)
    *outs, lse = pl.pallas_call(
        partial(attend_kernel, grouped),
        grid=(slots,),
        in_specs=[part(0), part(slots), part(2 * slots), whole],
        out_specs=[pl.BlockSpec((HEAD, span), lambda h: (h, 0))] * count
        + [pl.BlockSpec((1, 1, length), lambda h: (h, 0, 0))],
        out_shape=[jax.ShapeDtypeStruct((slots * HEAD, span), BF)] * count
        + [jax.ShapeDtypeStruct((slots, 1, length), F32)],
        compiler_params=pltpu.CompilerParams(vmem_limit_bytes=40 * 2**20),
        cost_estimate=pl.CostEstimate(
            flops=42 * slots * length * length * HEAD,
            bytes_accessed=4 * length * length + 8 * slots * HEAD * length,
            transcendentals=slots * length * length,
        ),
    )(mixed, mixed, mixed, bias)
    return outs, lse


def attend_back(mixed, grads, bias, lse, slots, grouped):
    length = mixed.shape[1]
    part = lambda first: pl.BlockSpec((HEAD, length), lambda h: (first + h, 0))
    whole = pl.BlockSpec((length, length), lambda h: (0, 0))
    count, span = (4, length // 4) if grouped else (1, length)
    return pl.pallas_call(
        partial(attend_back_kernel, grouped),
        grid=(slots,),
        in_specs=[
            part(0),
            part(slots),
            part(2 * slots),
            whole,
            pl.BlockSpec((1, 1, length), lambda h: (h, 0, 0)),
        ]
        + [pl.BlockSpec((HEAD, span), lambda h: (h, 0))] * count,
        out_specs=pl.BlockSpec(mixed.shape, lambda h: (0, 0)),
        out_shape=jax.ShapeDtypeStruct(mixed.shape, BF),
        scratch_shapes=[pltpu.VMEM((HEAD, length), F32), pltpu.VMEM((HEAD, length), F32)],
        compiler_params=pltpu.CompilerParams(vmem_limit_bytes=40 * 2**20),
        cost_estimate=pl.CostEstimate(
            flops=48 * slots * length * length * HEAD,
            bytes_accessed=4 * length * length + 14 * slots * HEAD * length,
            transcendentals=slots * length * length,
        ),
    )(mixed, mixed, mixed, bias, lse, *grads)


TOPS = (0, 2, 1, 3)
LOWS = (0, 1, 2, 3)


def kernel_call(kernel, member, inputs, outputs, scratch=()):
    count = len(inputs)
    size = sum(x.size * x.dtype.itemsize for x in inputs)
    size += sum(x.size * x.dtype.itemsize for x in outputs)
    return pl.pallas_call(
        kernel,
        in_specs=[pl.BlockSpec(memory_space=pltpu.SMEM)]
        + [pl.BlockSpec(memory_space=pltpu.VMEM)] * count,
        out_specs=[pl.BlockSpec(memory_space=pltpu.VMEM)] * len(outputs),
        out_shape=outputs,
        scratch_shapes=list(scratch),
        compiler_params=pltpu.CompilerParams(vmem_limit_bytes=48 * 2**20),
        cost_estimate=pl.CostEstimate(flops=0, bytes_accessed=size, transcendentals=0),
    )(member.reshape(1), *inputs)


def slab_places(member, rows, step, slab):
    found = []
    for part, order in enumerate((TOPS, LOWS)):
        for turn in order:
            owner = member ^ turn
            for block in (2 * part, 2 * part + 1):
                found.append((owner, block * rows + owner * step))
    return found


def sort_heads_kernel(slots, rows, step, slab, member_ref, *refs):
    *got, out_ref, whole = refs
    member = member_ref[0]
    width = whole.shape[0]
    high = slots * HEAD
    for turn in range(4):
        owner = member ^ turn
        at = jnp.minimum(owner * high, width - high)
        spare = (owner * high - at) // HEAD
        if turn == 0:
            pass
        for slot in range(slots):

            @pl.when(slot >= spare)
            def _(turn=turn, slot=slot, at=at):
                to = pl.multiple_of(at + slot * HEAD, HEAD)
                whole[pl.ds(to, HEAD), :] = got[turn][slot * HEAD : (slot + 1) * HEAD, :]

    line = lax.broadcasted_iota(jnp.int32, (slab, 1), 0)
    for index, (owner, at) in enumerate(slab_places(member, rows, step, slab)):
        rows_here = whole[pl.ds(pl.multiple_of(at, 16), slab), :]
        keep = (line < step) | (owner == 3)
        out_ref[index * slab : (index + 1) * slab, :] = jnp.where(
            keep, rows_here, jnp.zeros_like(rows_here)
        )


def split_heads_kernel(slots, rows, step, slab, member_ref, value_ref, *refs):
    *outs, whole = refs
    member = member_ref[0]
    width = whole.shape[0]
    high = slots * HEAD
    for index, (owner, at) in enumerate(slab_places(member, rows, step, slab)):
        first = index * slab
        whole[pl.ds(pl.multiple_of(at, 16), step), :] = value_ref[first : first + step, :]

        @pl.when(owner == 3)
        def _(first=first, at=at):
            to = pl.multiple_of(at + step, 16)
            whole[pl.ds(to, slab - step), :] = value_ref[first + step : first + slab, :]

    for turn in range(4):
        owner = member ^ turn
        at = jnp.minimum(owner * high, width - high)
        spare = owner * high - at
        line = lax.broadcasted_iota(jnp.int32, (high, 1), 0)
        rows_here = whole[pl.ds(pl.multiple_of(at, HEAD), high), :]
        outs[turn][...] = jnp.where(line >= spare, rows_here, jnp.zeros_like(rows_here))


def member_rows(refs, member, owner, cut, rows):
    if member is None:
        at = owner * rows
        return [
            (ref[at : at + cut, :].astype(F32), ref[at + cut : at + rows, :].astype(F32))
            for ref in refs
        ]
    turn = member ^ owner
    twin = (turn & 1) * 2 + turn // 2
    found = []
    for ref in refs:
        top = ref[pl.ds(pl.multiple_of(twin * cut, 16), cut), :]
        low = ref[pl.ds(pl.multiple_of(4 * cut + turn * (rows - cut), 16), rows - cut), :]
        found.append((top.astype(F32), low.astype(F32)))
    return found


def blocks_into(out_ref, lines, value, block, padded):
    for index in range(value.shape[1] // padded):
        out_ref[lines, index * block : (index + 1) * block] = value[
            :, index * padded : index * padded + block
        ]


def finish_attn_kernel(slots, cut, total, _, left_ref, right_ref, out_ref):
    member = None
    rows = out_ref.shape[0]
    width = out_ref.shape[1] // 3
    high = slots * HEAD
    held = left_ref.shape[0] // 4
    for owner in range(4):
        start = min(owner * high, width - high)
        spare = owner * high - start
        (left, right) = member_rows((left_ref, right_ref), member, owner, cut, held)
        for lines, first, size in ((0, 0, cut), (1, cut, rows - cut)):
            shared = left[lines].shape[1] * 2 - total
            both = jnp.concatenate([left[lines], right[lines][:, shared:]], axis=1)
            for third in range(3):
                to = third * width + start + spare
                out_ref[first : first + size, to : to + high - spare] = both[
                    :size, third * high + spare : (third + 1) * high
                ]


def finish_proj_kernel(step, slab, cut, total, padded, _, left_ref, right_ref, out_ref):
    member = None
    block = out_ref.shape[1] // 4
    for owner in range(4):
        size = slab if owner == 3 else step
        (left, right) = member_rows((left_ref, right_ref), member, owner, cut, slab)
        for lines, first, count in ((0, 0, cut), (1, cut, size - cut)):
            shared = left[lines].shape[1] * 2 - total
            both = jnp.concatenate([left[lines], right[lines][:, shared:]], axis=1)[:count]
            at = owner * step + first
            blocks_into(out_ref, slice(at, at + count), both, block, padded)


def finish_in_kernel(cut, padded, _, value_ref, out_ref):
    member = None
    rows = out_ref.shape[0]
    part = out_ref.shape[1] // 16
    for owner in range(4):
        ((top, low),) = member_rows((value_ref,), member, owner, cut, padded)
        for block in range(4):
            to = (block * 4 + owner) * part
            out_ref[:cut, to : to + part] = top[:, block * padded : block * padded + part]
            out_ref[cut:, to : to + part] = low[
                : rows - cut, block * padded : block * padded + part
            ]


def finish_out_kernel(cut, padded, _, value_ref, out_ref):
    member = None
    rows = out_ref.shape[0] // 4
    block = out_ref.shape[1] // 4
    for owner in range(4):
        ((top, low),) = member_rows((value_ref,), member, owner, cut, padded)
        at = owner * rows
        blocks_into(out_ref, slice(at, at + cut), top, block, padded)
        blocks_into(out_ref, slice(at + cut, at + rows), low[: rows - cut], block, padded)


def expand_kernel(padded, _, *refs):
    half = len(refs) // 2
    for value_ref, out_ref in zip(refs[:half], refs[half:]):
        block = value_ref.shape[1] // 4
        out_ref[...] = jnp.zeros_like(out_ref)
        for index in range(4):
            out_ref[:, index * padded : index * padded + block] = value_ref[
                :, index * block : (index + 1) * block
            ]


def edge_kernel(padded, section_ref, mine_ref, other_ref, edge_ref):
    block = edge_ref.shape[4] // 4
    wide = 4 * padded
    for side, refs in enumerate(((mine_ref, other_ref), (other_ref, mine_ref))):

        @pl.when(section_ref[0] == side)
        def _(side=side, refs=refs):
            for index, ref in enumerate(refs):
                value = ref[:, side * wide : (side + 1) * wide].astype(F32)
                blocks_into(edge_ref.at[0, index, 0], slice(None), value, block, padded)


def order_kernel(forth, place_ref, value_ref, out_ref):
    n = value_ref.shape[0] // 8
    at = 0
    for part, order in enumerate((TOPS, LOWS)):
        for turn in order:
            rows = pl.ds(pl.multiple_of(((place_ref[0] ^ turn) * 2 + part) * n, n), n)
            if forth:
                out_ref[at : at + n, :] = value_ref[rows, :]
            else:
                out_ref[rows, :] = value_ref[at : at + n, :]
            at += n


def deal_kernel(whole_in, whole_out, places_ref, *refs):
    place = places_ref[0]
    count = 1 if whole_in else 4
    inputs, outs = refs[:count], refs[count:]
    size = inputs[0].shape[0] // (4 if whole_in else 1)
    for turn in range(4):
        at = pl.multiple_of((place ^ turn) * size, size)
        if whole_in:
            outs[turn][...] = inputs[0][pl.ds(at, size), :]
        elif whole_out:
            outs[0][pl.ds(at, size), :] = inputs[turn][...]
        else:
            for owner in range(4):

                @pl.when((place ^ turn) == owner)
                def _(turn=turn, owner=owner):
                    outs[turn][...] = inputs[owner][...]


def join_kernel(_, own, near_a, near_b, far_a, far_b, *out_refs):
    n, m = near_a.shape[0], near_b.shape[0]
    at = 0
    for part, first, size in (
        (own, 0, n),
        (near_a, 0, n),
        (far_a, 0, 2 * n),
        (own, n, m),
        (near_b, 0, m),
        (far_b, 0, 2 * m),
    ):
        column = 0
        for out_ref in out_refs:
            width = out_ref.shape[1]
            out_ref[at : at + size, :] = part[first : first + size, column : column + width]
            column += width
        at += size


def place_kernel(widths, member_ref, *refs):
    pieces, outs = refs[:4], refs[4:]
    rows = pieces[0].shape[0]
    for turn in range(4):
        at = pl.multiple_of((member_ref[0] ^ turn) * rows, 16)
        column = 0
        for width, out_ref in zip(widths, outs):
            out_ref[pl.ds(at, rows), :] = pieces[turn][:, column : column + width]
            column += width


def total_kernel(place_ref, *refs):
    pieces, out_ref = refs[:4], refs[4]
    for place in range(4):

        @pl.when(place_ref[0] == place)
        def _(place=place):
            first, second, third, fourth = (pieces[place ^ turn][...] for turn in range(4))
            out_ref[...] = ((first + second) + third) + fourth


def same_kernel(*refs):
    pass


def tie(value, *others):
    any_place = pl.BlockSpec(memory_space=pl.ANY)
    return pl.pallas_call(
        same_kernel,
        in_specs=[any_place] * (1 + len(others)),
        out_specs=any_place,
        out_shape=jax.ShapeDtypeStruct(value.shape, value.dtype),
        input_output_aliases={0: 0},
        cost_estimate=pl.CostEstimate(flops=0, bytes_accessed=0, transcendentals=0),
    )(value, *others)


def body(
    replicas,
    shards,
    boundary,
    segments,
    attn_weight,
    proj_weight,
    fc_in_weight,
    fc_out_weight,
    norm_gains,
    vector_bias,
    fc_in_bias,
):
    sub = shards // replicas
    team = replicas * sub
    fast = replicas == 4 and sub == 1
    team_axes = ("replica", "sub")
    row_axes = ("seq", "sub")
    chip_axes = ("replica", "seq", "sub")
    section = lax.axis_index("section")
    first = section == 0
    member = lax.axis_index(team_axes)
    local = boundary.shape[3]
    width = boundary.shape[4]
    hidden = fc_in_bias.shape[1]
    n = local // 2
    length = segments.shape[2]
    half = length // 2
    slots = -(-HEADS // team)
    heads_width = slots * HEAD
    hid = hidden // team
    block = width // 4
    padded = -(-block // 32) * 32 if fast else block
    wide = 4 * padded
    mask = None
    if fast:
        mask = (jnp.arange(wide) % padded < block).astype(F32)
    mixed_rows = -(-3 * heads_width // 128) * 128 if fast else 3 * heads_width
    attn_half = -(-mixed_rows // 256) * 128
    proj_half = -(-wide // 256) * 128

    def head_start(index):
        return jnp.minimum(index * slots, HEADS - slots)

    def spare_heads(index):
        return min(max(index * slots - (HEADS - slots), 0), slots)

    start = head_start(member) * HEAD

    def cross(value, pairs=SWAP):
        return lax.ppermute(value, "section", pairs)

    def side(value):
        return lax.ppermute(value, "replica", SIDE)

    def across(value):
        return lax.ppermute(value, "replica", ACROSS)

    def corner(value):
        return lax.ppermute(value, "replica", CORNER)

    def pick(a, b):
        return jnp.where(first, a, b)

    def halves(value, half, axis):
        size = value.shape[axis]
        left = lax.slice_in_dim(value, 0, half, axis=axis)
        right = lax.slice_in_dim(value, size - half, size, axis=axis)
        return pick(left, right), pick(right, left)

    def spaced(vector):
        if not fast:
            return vector
        parts = vector.reshape(-1, 4, block)
        parts = jnp.pad(parts, ((0, 0), (0, 0), (0, padded - block)))
        return parts.reshape(vector.shape[:-1] + (wide,))

    def dense(vector):
        if not fast:
            return vector
        return vector.reshape(vector.shape[:-1] + (4, padded))[..., :block].reshape(
            vector.shape[:-1] + (width,)
        )

    def flat(p, z):
        return p * shards + z

    rounds = []
    for turn in range(2):
        pairs = []
        for p in range(replicas):
            for z in range(shards):
                slot = z // (shards // 2)
                h = turn if slot == 0 else 1 - turn
                j = 2 * (z % (shards // 2)) + h
                target = flat(j // sub, p * sub + j % sub)
                pairs.append((flat(p, z), target))
        rounds.append(pairs)
    place = lax.axis_index(row_axes)
    early = place < shards // 2
    even = member % 2 == 0

    def to_team_far(value):
        top, low = value[:n], value[n:]
        one = lax.ppermute(jnp.where(early, top, low), chip_axes, rounds[0])
        two = lax.ppermute(jnp.where(early, low, top), chip_axes, rounds[1])
        return jnp.concatenate([jnp.where(even, one, two), jnp.where(even, two, one)])

    def from_team_far(value):
        top, low = value[:n], value[n:]
        one = lax.ppermute(
            jnp.where(even, top, low), chip_axes, [(b, a) for a, b in rounds[0]]
        )
        two = lax.ppermute(
            jnp.where(even, low, top), chip_axes, [(b, a) for a, b in rounds[1]]
        )
        return jnp.concatenate([jnp.where(early, one, two), jnp.where(early, two, one)])

    plane = lax.axis_index("seq")

    def turned(pieces, axis):
        own, *others = pieces
        return [own] + [
            lax.ppermute(x, axis, pairs) for x, pairs in zip(others, (SIDE, ACROSS, CORNER))
        ]

    def dealt(place, pieces, whole_in, whole_out):
        rows, columns = pieces[0].shape
        if whole_in:
            outs = [jax.ShapeDtypeStruct((rows // 4, columns), BF)] * 4
        elif whole_out:
            outs = [jax.ShapeDtypeStruct((rows * 4, columns), BF)]
        else:
            outs = [jax.ShapeDtypeStruct((rows, columns), BF)] * 4
        return kernel_call(partial(deal_kernel, whole_in, whole_out), place, pieces, outs)

    def to_team(value):
        if not fast:
            return to_team_far(value)
        pieces = turned(dealt(member, [value], True, False), "replica")
        pieces = turned(dealt(plane ^ member, pieces, False, False), "seq")
        return dealt(plane, pieces, False, True)[0]

    def from_team(value):
        if not fast:
            return from_team_far(value)
        pieces = turned(dealt(plane, [value], True, False), "seq")
        pieces = turned(dealt(plane ^ member, pieces, False, False), "replica")
        return dealt(member, pieces, False, True)[0]

    if fast:
        order_a = [member, member ^ 2, member ^ 1, member ^ 3]
        order_b = [member, member ^ 1, member ^ 2, member ^ 3]
    else:
        order_a = order_b = list(range(team))

    def gather_near(value, cut, widths=None):
        a, b = value[:cut], value[cut:]
        if not fast:
            whole = jnp.concatenate(
                [
                    lax.all_gather(a, team_axes, axis=0, tiled=True),
                    lax.all_gather(b, team_axes, axis=0, tiled=True),
                ]
            )
            return whole, whole
        near_a, near_b = across(a), side(b)
        return gather_far(value, cut, near_a, near_b, widths), near_b

    def gather_far(value, cut, near_a, near_b, widths=None):
        a, b = value[:cut], value[cut:]
        far_a = side(jnp.concatenate([a, near_a]))
        far_b = across(jnp.concatenate([b, near_b]))
        outs = [
            jax.ShapeDtypeStruct((4 * value.shape[0], width), value.dtype)
            for width in widths or [value.shape[1]]
        ]
        parts = [value, near_a, near_b, far_a, far_b]
        outs = kernel_call(join_kernel, member, parts, outs)
        return outs if widths else outs[0]

    def gather(value, cut):
        return gather_near(value, cut)[0]

    def gather_many(values, cut):
        whole = jnp.concatenate(values, axis=1)
        return gather_near(whole, cut, [value.shape[1] for value in values])[0]

    def gather_direct(value, widths=None):
        pieces = [value, side(value), across(value), corner(value)]
        widths = widths or [value.shape[1]]
        rows = 4 * value.shape[0]
        outs = [jax.ShapeDtypeStruct((rows, width), value.dtype) for width in widths]
        return kernel_call(partial(place_kernel, widths), member, pieces, outs)

    def edge_of(value):
        return lax.slice(value, (0, 0), (16, 128))

    def ordered(forth, value):
        out = jax.ShapeDtypeStruct(value.shape, value.dtype)
        return kernel_call(partial(order_kernel, forth), member, [value], [out])[0]

    def gather_late(value):
        if not fast:
            return gather(value, n)
        whole = lax.all_gather(value, "replica", axis=0, tiled=True)
        return ordered(True, whole)

    def scatter_late(value):
        if not fast:
            return scatter(value)
        whole = ordered(False, value)
        return lax.psum_scatter(whole, "replica", scatter_dimension=0, tiled=True)


    def scatter(value, got=None):
        middle_row = value.shape[0] // 2
        a, b = value[:middle_row], value[middle_row:]
        if not fast:
            return jnp.concatenate(
                [
                    lax.psum_scatter(a.astype(F32), team_axes, scatter_dimension=0, tiled=True),
                    lax.psum_scatter(b.astype(F32), team_axes, scatter_dimension=0, tiled=True),
                ]
            )
        m = middle_row // 4
        got_a, got_b = got or scatter_first(value)
        sent_a = (a[m : 2 * m].astype(F32) + got_a[m:]).astype(BF)
        sent_b = (b[m : 2 * m].astype(F32) + got_b[m:]).astype(BF)
        last_a, last_b = across(sent_a), side(sent_b)
        sum_a = a[:m].astype(F32) + got_a[:m] + last_a
        sum_b = b[:m].astype(F32) + got_b[:m] + last_b
        return jnp.concatenate([sum_a, sum_b])

    def scatter_first(value):
        middle_row = value.shape[0] // 2
        m = middle_row // 4
        return side(value[2 * m : middle_row]), across(value[middle_row + 2 * m :])

    if fast:
        rows = width // replicas
        slab = -(-rows // 64) * 16
        step = (rows - slab) // 3
        cut = padded // 2
        sorted_heads = jax.ShapeDtypeStruct((16 * slab, 2 * n), BF)
        one = jax.ShapeDtypeStruct((heads_width, 2 * n), BF)
        scratch = [pltpu.VMEM((width, 2 * n), BF)]

    def heads_to_tokens(values):
        if fast:
            own, near, over, far = values
            got = [own, side(near), across(over), corner(far)]
            kernel = partial(sort_heads_kernel, slots, rows, step, slab)
            return kernel_call(kernel, member, got, [sorted_heads], scratch)[0]
        pieces = values[0].reshape(heads_width, 2, team, n).transpose(2, 0, 1, 3)
        got = lax.all_to_all(pieces, team_axes, 0, 0, tiled=True)
        got = got.reshape(team, heads_width, 2 * n)
        pieces = []
        for index in range(team):
            spare = spare_heads(index) * HEAD
            if spare < heads_width:
                pieces.append(got[index, spare:])
        return jnp.concatenate(pieces)

    def tokens_to_heads(value):
        if fast:
            kernel = partial(split_heads_kernel, slots, rows, step, slab)
            own, near, over, far = kernel_call(kernel, member, [value], [one] * 4, scratch)
            return [own, side(near), across(over), corner(far)]

        def of(index):
            return lax.dynamic_slice_in_dim(value, head_start(index) * HEAD, heads_width, 0)

        pieces = jnp.stack([of(index) for index in range(team)])
        got = lax.all_to_all(pieces, team_axes, 0, 0, tiled=True)
        got = got.reshape(team, heads_width, 2, n).transpose(1, 2, 0, 3)
        whole = got.reshape(heads_width, length)
        spare = member * slots - head_start(member)
        lines = lax.broadcasted_iota(jnp.int32, (heads_width, 1), 0)
        return [jnp.where(lines >= spare * HEAD, whole, jnp.zeros_like(whole))]

    def head_columns(weight):
        return [
            lax.dynamic_slice_in_dim(weight, third * width + start, heads_width, 1)
            for third in range(3)
        ]

    if fast:
        hid_part = hid // replicas
        more = padded - rows
        own_attn = jnp.concatenate(head_columns(attn_weight[0]), axis=1)
        own_attn = jnp.pad(own_attn, ((0, more), (0, mixed_rows - 3 * heads_width)))
        own_in = jnp.concatenate(
            [
                jnp.pad(
                    lax.dynamic_slice_in_dim(
                        fc_in_weight[0], part * hid + member * hid_part, hid_part, 1
                    ),
                    ((0, more), (0, padded - hid_part)),
                )
                for part in range(replicas)
            ],
            axis=1,
        )
        own_out = lax.dynamic_slice_in_dim(fc_out_weight[0], member * hid_part, hid_part, 0)
        own_proj = lax.dynamic_slice_in_dim(proj_weight[0], member * step, slab, 0)
        own_out, own_proj = kernel_call(
            partial(expand_kernel, padded),
            member,
            [own_out, own_proj],
            [jax.ShapeDtypeStruct((hid_part, wide), BF), jax.ShapeDtypeStruct((slab, wide), BF)],
        )
        own_out = jnp.pad(own_out, ((0, padded - hid_part), (0, 0)))

        def gathered(piece):
            return lax.all_gather(piece, "seq", axis=0, tiled=True)

        def full(mine):
            other = cross(mine)
            return pick(mine, other), pick(other, mine)

        def spread(pair):
            got = cross(pair[1])
            return pick(pair[0], got), pick(got, pair[0])

        attn_pieces = spread(halves(own_attn, attn_half, 1))
        fc_pieces = spread((pick(own_in, own_out), pick(own_out, own_in)))
        shared = 2 * attn_half - mixed_rows
        attn_got = [gathered(attn_pieces[0])]
        proj_got = []
        fc_got = []
        proj_whole = []

        def fetch_proj(after):
            proj_got.append(gathered(tie(own_proj, after)))

        def fetch_fc(layer, after):
            fc_got.append(gathered(tie(fc_pieces[layer], after)))

        def fetch_attn(after):
            attn_got.append(gathered(tie(attn_pieces[1], after)))

        def get_attn(layer, after):
            left, right = full(tie(attn_got[layer], after))
            return jnp.concatenate([left, right[:, shared:]], axis=1)

        def get_proj(layer, near=None, after=None):
            if layer == 0:
                mine = tie(proj_got[0], near)
                near = across(mine[: 2 * slab]), side(mine[2 * slab :])
                near = [tie(value, after) for value in near]
                mine = gather_far(mine, 2 * slab, *near)
                other = cross(mine)
                proj_whole.extend([pick(mine, other), pick(other, mine)])
            return proj_whole[layer]

        def get_fc(layer, after):
            return full(tie(fc_got[layer], after))

        def hid_of(vector):
            mine = lax.dynamic_slice_in_dim(
                vector.reshape(replicas, replicas, hid_part), member, 1, 1
            )
            return jnp.pad(mine[:, 0], ((0, 0), (0, padded - hid_part))).reshape(wide)

        def hid_into(vector):
            zeros = jnp.zeros((replicas, replicas, hid_part), F32)
            return lax.dynamic_update_slice_in_dim(
                zeros, vector.reshape(replicas, 1, padded)[..., :hid_part], member, 1
            ).reshape(hidden)

    else:

        def both(value):
            other = cross(value)
            return pick(value, other), pick(other, value)

        def weights_of(layer):
            def whole(weight):
                return lax.all_gather(both(weight[0])[layer], row_axes, axis=0, tiled=True)

            w_attn = jnp.concatenate(head_columns(whole(attn_weight)), axis=1)
            w_proj = whole(proj_weight)
            w_in = lax.dynamic_slice_in_dim(whole(fc_in_weight), member * hid, hid, 1)
            w_out = lax.dynamic_slice_in_dim(whole(fc_out_weight), member * hid, hid, 0)
            return w_attn, w_proj, w_in, w_out

        whole_weights = [weights_of(0), weights_of(1)]

        def fetch_proj(after):
            pass

        def fetch_fc(layer, after):
            pass

        fetch_attn = fetch_proj

        def get_attn(layer, after):
            return whole_weights[layer][0]

        def get_proj(layer, *others):
            return whole_weights[layer][1]

        def get_fc(layer, after):
            return whole_weights[layer][2:]

        def hid_of(vector):
            return lax.dynamic_slice_in_dim(vector, member * hid, hid, 0)

        def hid_into(vector):
            return lax.dynamic_update_slice_in_dim(
                jnp.zeros((hidden,), F32), vector, member * hid, 0
            )

    def heads_into(vector):
        return lax.dynamic_update_slice_in_dim(jnp.zeros((width,), F32), vector, start, 0)

    block_0, block_1 = boundary[0, 0, 0], boundary[0, 1, 0]
    if fast:
        block_0, block_1 = kernel_call(
            partial(expand_kernel, padded),
            member,
            [block_0, block_1],
            [jax.ShapeDtypeStruct((local, wide), BF)] * 2,
        )
    kept = pick(block_0, block_1)
    got = cross(pick(block_1, block_0))
    source = to_team(pick(kept, got))
    cotangent = pick(got, kept)
    vectors = jnp.concatenate([norm_gains[0].ravel(), vector_bias[0].ravel(), fc_in_bias[0]])
    other_vectors = cross(vectors)
    vectors = (pick(vectors, other_vectors), pick(other_vectors, vectors))

    ids = lax.dynamic_index_in_dim(segments, section, 0, keepdims=False)[0]
    swapped = [
        (flat(p, z * sub + k), flat(z, p * sub + k))
        for p in range(replicas)
        for z in range(replicas)
        for k in range(sub)
    ]
    ids = lax.ppermute(ids, chip_axes, swapped).reshape(2, team, n)
    places, names = [], []
    for chunk, order in enumerate((order_a, order_b)):
        for index in order:
            places.append(chunk * half + index * n + jnp.arange(n, dtype=jnp.int32))
            names.append(lax.dynamic_index_in_dim(ids[chunk], index, 0, keepdims=False))
    if fast:
        places, names = [], []
        ids = ids.reshape(2, 2, team, n // 2)
        for chunk, order in enumerate((order_a, order_b)):
            for index in order:
                for part in range(2):
                    at = chunk * half + part * (half // 2) + index * (n // 2)
                    places.append(at + jnp.arange(n // 2, dtype=jnp.int32))
                    names.append(
                        lax.dynamic_index_in_dim(ids[chunk, part], index, 0, keepdims=False)
                    )
    places, names = jnp.concatenate(places), jnp.concatenate(names)
    allowed = (names[:, None] == names[None, :]) & (places[:, None] <= places[None, :])
    bias = jnp.where(allowed, 0.0, MASKED).astype(F32)

    def parameters(layer):
        vector = vectors[layer]
        lines = vector[: 8 * width].reshape(8, width)
        query_bias = lax.dynamic_slice_in_dim(lines[3], start, heads_width, 0)
        value_bias = lax.dynamic_slice_in_dim(lines[4], start, heads_width, 0)
        lines = spaced(lines)
        gains, biases = lines[:2], lines[2:]
        hid_bias = hid_of(vector[8 * width :])
        mixed_bias = jnp.concatenate([query_bias, jnp.zeros_like(query_bias), value_bias])
        mixed_bias = jnp.pad(mixed_bias, (0, mixed_rows - mixed_bias.shape[0]))
        return gains, biases, hid_bias, mixed_bias

    def enter(layer, value):
        gains, biases, _, _ = parameters(layer)
        normed = (norm_stats(value, mask, width)[0] * gains[0] + biases[0]).astype(BF)
        return gather_near(normed, n)

    def mix(layer, normed, w_attn, *others):
        mixed_bias = parameters(layer)[3]
        if fast and others:
            mixed_bias = tie(mixed_bias, *others)
        return (dot(w_attn, normed, (0, 1)) + mixed_bias[:, None]).astype(BF)

    def forward(layer, value, normed, mixed, w_proj, hold):
        gains, biases, hid_bias, _ = parameters(layer)
        proj_bias = tie(biases[3], fc_got[0]) if fast and layer == 0 else biases[3]
        attended, lse = attend(mixed, bias, slots, fast)
        if layer == 0:
            w_proj.append(get_proj(0, near, lse))
        w_proj = w_proj[layer]
        attended = heads_to_tokens(attended)
        middle = value + dot(attended, w_proj, (0, 0)) + proj_bias
        gain = hold(gains[1])
        normed_two = (norm_stats(middle, mask, width)[0] * gain + biases[4]).astype(BF)
        w_in, w_out = get_fc(layer, normed_two)
        normed_two = gather(normed_two, n)
        activated, slope = gelu_pair(dot(normed_two, w_in, (1, 0)) + hid_bias)
        activated, slope = lax.optimization_barrier((activated.astype(BF), slope.astype(BF)))
        kept = (value, normed, mixed, lse, attended, middle, normed_two, activated, slope)
        return kept, (w_in, w_out)

    def leave(layer, middle, activated, w_out):
        return dot(activated, w_out, (1, 0)).astype(BF)

    ones = lax.optimization_barrier(jnp.ones((16, length), BF))

    def backward(layer, grad_out, grad_low, kept, weights, fillers):
        value, normed, mixed, lse, attended, middle, normed_two, activated, slope = kept
        w_attn, w_proj, w_in, w_out = weights
        gains = parameters(layer)[0]
        low_sum = jnp.sum(grad_out, axis=0)
        grad_pre = (dot(grad_low, w_out, (1, 1)) * slope).astype(BF)
        part = dot(grad_pre, w_in, (1, 1)).astype(BF)
        fillers[0](part)
        grad_two = scatter(part)
        if fast:
            sent = dot(pick(activated, normed_two), pick(grad_low, grad_pre), (0, 0))
            sent = cross(sent.astype(BF))
            fc_pair = (pick(normed_two, activated), pick(grad_pre, grad_low), sent)
        else:
            fc_pair = (
                dot(normed_two, grad_pre, (0, 0)).astype(BF),
                dot(activated, grad_low, (0, 0)).astype(BF),
            )
        fillers[1](part)
        hid_sum = dot(ones, grad_pre, (1, 0))[0]
        gain = fillers[4](gains[1])
        grad_norm, gain_two, shift_two = norm_back(grad_two, middle, gain, mask, width)
        grad_middle = grad_out + grad_norm
        grad_branch = grad_middle.astype(BF)
        branch_sum = jnp.sum(grad_branch.astype(F32), axis=0)
        grad_attended = dot(w_proj, grad_branch, (1, 1)).astype(BF)
        grad_attended = tokens_to_heads(grad_attended)
        own, other = halves(grad_branch, proj_half, 1)
        if fast:
            sent = cross(dot(attended, other, (1, 0)).astype(BF))
            fc_total = (dot(fc_pair[0], fc_pair[1], (0, 0)) + fc_pair[2]).astype(BF)
            proj_total = (dot(attended, own, (1, 0)) + sent).astype(BF)
        else:
            fc_total = fc_pair
            proj_total = dot(attended, grad_branch, (1, 0)).astype(BF)
        fillers[2](grad_attended[-1], fc_total, proj_total)
        lse = fillers[3](lse, proj_total)
        grad_mixed = attend_back(mixed, grad_attended, bias, lse, slots, fast)
        part = dot(grad_mixed, w_attn, (0, 1)).astype(BF)
        grad_one = scatter(part)
        own, other = halves(grad_mixed, attn_half, 0)
        if fast:
            attn_pair = (own, cross(dot(normed, other, (0, 1)).astype(BF)))
            attn_total = (dot(normed, attn_pair[0], (0, 1)) + attn_pair[1]).astype(BF)
        else:
            attn_total = dot(normed, grad_mixed, (0, 1)).astype(BF)
        mixed_sum = jnp.sum(grad_mixed.astype(F32), axis=1)
        gain = fillers[5](gains[0])
        grad_norm, gain_one, shift_one = norm_back(grad_one, value, gain, mask, width)
        grad_in = grad_middle + grad_norm
        query_sum = heads_into(mixed_sum[:heads_width])
        value_sum = heads_into(mixed_sum[2 * heads_width : 3 * heads_width])
        lines = dense(
            jnp.stack([gain_one, gain_two, shift_one, branch_sum, shift_two, low_sum])
        )
        small = jnp.concatenate(
            [
                lines[:3].ravel(),
                query_sum,
                value_sum,
                lines[3:].ravel(),
                hid_into(hid_sum),
            ]
        )
        return grad_in, small, fc_total, proj_total, attn_total, grad_mixed

    if fast:

        proj_cut = (slab // 32) * 16

        def over_planes(total):
            return lax.psum_scatter(total, "seq", scatter_dimension=0, tiled=True)

        def both(mine_0, mine_1):
            return (mine_0, cross(mine_0, [(1, 0)])), (mine_1, cross(mine_1, [(0, 1)]))

        def finish(kernel, pairs, shape):
            (mine_0, other_0), (mine_1, other_1) = pairs
            left, right = pick(mine_0, other_1), pick(other_0, mine_1)
            out = jax.ShapeDtypeStruct(shape, F32)
            return kernel_call(kernel, member, [left, right], [out])[0]

        def finish_fc(pairs):
            (mine_0, other_0), (mine_1, other_1) = pairs
            left, right = pick(mine_0, other_1), pick(other_0, mine_1)
            w_in = kernel_call(
                partial(finish_in_kernel, cut, padded),
                member,
                [left],
                [jax.ShapeDtypeStruct((rows, hidden), F32)],
            )[0]
            w_out = kernel_call(
                partial(finish_out_kernel, cut, padded),
                member,
                [right],
                [jax.ShapeDtypeStruct((hid, width), F32)],
            )[0]
            return w_in, w_out

        def reduce_small(small):
            total = pick(small[0], small[1]) + cross(pick(small[1], small[0]))
            total = total.reshape(-1, 128)
            out = [jax.ShapeDtypeStruct(total.shape, F32)]
            total = kernel_call(total_kernel, member, turned([total] * 4, "replica"), out)[0]
            total = kernel_call(total_kernel, plane, turned([total] * 4, "seq"), out)[0]
            return total.reshape(-1)

    held = {}

    def nothing(*_):
        pass

    def same(value, *_):
        return value

    values = source.astype(F32)
    fetch_proj(source)
    normed, near = enter(0, values)
    fetch_fc(0, near)
    attn_weights = [get_attn(0, source)]
    cotangent = to_team(cotangent)
    mixed = mix(0, normed, attn_weights[0], cotangent)
    proj_weights = []
    fetch_attn(mixed)
    fetch_fc(1, mixed)
    kept_0, fc_0 = forward(0, values, normed, mixed, proj_weights, same)
    part = leave(0, kept_0[5], kept_0[7], fc_0[1])
    attn_weights.append(get_attn(1, part))
    passed = kept_0[5] + scatter(part) + parameters(0)[1][5]
    values = passed.astype(BF).astype(F32)
    normed, near = enter(1, values)
    mixed = mix(1, normed, attn_weights[1])
    proj_weights.append(get_proj(1))
    grad_low = gather_late(tie(cotangent, edge_of(mixed)) if fast else cotangent)

    def hold_low(value):
        return value

    kept_1, fc_1 = forward(1, values, normed, mixed, proj_weights, hold_low)
    weights_0 = (attn_weights[0], proj_weights[0], *fc_0)
    weights_1 = (attn_weights[1], proj_weights[1], *fc_1)

    def finish_forward(part):
        held["out"] = scatter_late(leave(1, kept_1[5], kept_1[7], fc_1[1]))

    def start_fc(layer):
        def start(grad_attended, fc_total, proj_total):
            if fast:
                held[layer] = over_planes(fc_total)

        return start

    fillers = (nothing, finish_forward, start_fc(1), same, same, same)
    grad, small_1, fc_1, proj_1, attn_1, _ = backward(
        1, cotangent.astype(F32), grad_low, kept_1, weights_1, fillers
    )
    out = (kept_1[5] + held["out"] + parameters(1)[1][5]).astype(BF)
    grad = grad.astype(BF)
    grad_low = gather(grad, n)
    fillers = (nothing, nothing, start_fc(0), same, same, same)
    if fast:
        attn_1 = over_planes(attn_1)

        held["fc_1"] = lax.all_gather(held[1], "replica", axis=0, tiled=True)

        held["attn_1"] = lax.all_gather(attn_1, "replica", axis=0, tiled=True)

        def hold_sums(value, proj_0):
            held["proj"] = whole = jnp.concatenate([proj_0, proj_1], axis=1)
            held["got"] = scatter_first(whole)
            return tie(value, *held["got"])

        def hold_attn(value):
            return tie(value, held["attn_1"])

        def hold_gathered(value):
            return tie(value, held["fc_1"])

        fillers = (nothing, nothing, start_fc(0), hold_sums, hold_gathered, hold_attn)
    grad, small_0, fc_0, proj_0, attn_0, grad_mixed = backward(
        0, grad.astype(F32), grad_low, kept_0, weights_0, fillers
    )
    grad = grad.astype(BF)
    if fast:
        proj = scatter(held["proj"], held["got"]).astype(BF)
        proj = over_planes(proj)
        attn_last = attn_0
        attn_0 = over_planes(attn_0)
        mine = from_team(jnp.concatenate([grad, out], axis=1))
        edge = kernel_call(
            partial(edge_kernel, padded),
            section,
            [mine, cross(mine)],
            [jax.ShapeDtypeStruct((1, 2, 1, local, width), F32)],
        )[0]
        fc_0 = lax.all_gather(tie(held[0], edge_of(attn_last)), "replica", axis=0, tiled=True)
        fc = both(fc_0, held["fc_1"])
        attn = both(gather_direct(attn_0)[0], held["attn_1"])
        proj = both(*gather_direct(proj, [proj_half, proj_half]))
    else:
        out, grad = from_team(out), from_team(grad)
        got_out, got_grad = cross(out, [(0, 1)]), cross(grad, [(1, 0)])
        edge = jnp.stack([pick(grad, got_out), pick(got_grad, out)]).astype(F32)
    edge = edge.reshape(1, 2, 1, local, width)
    if fast:
        in_sum, out_sum = finish_fc(fc)
        kernel = partial(finish_proj_kernel, step, slab, proj_cut, wide, padded)
        proj_sum = finish(kernel, proj, (rows, width))
        kernel = partial(finish_attn_kernel, slots, cut, mixed_rows)
        attn_sum = finish(kernel, attn, (rows, 3 * width))
        small = reduce_small((small_0, small_1))
    else:

        def summed(make, after):
            parts = [lax.optimization_barrier((make(layer), after))[0] for layer in range(2)]
            mine = pick(parts[0], parts[1]) + cross(pick(parts[1], parts[0]))
            mine = lax.psum_scatter(mine, row_axes, scatter_dimension=0, tiled=True)
            return lax.psum(mine.astype(F32), ("replica",))

        def attn_whole(layer):
            value = (attn_0, attn_1)[layer]
            zeros = jnp.zeros((width, width), BF)
            parts = [value[:, i * heads_width : (i + 1) * heads_width] for i in range(3)]
            return jnp.concatenate(
                [lax.dynamic_update_slice_in_dim(zeros, x, start, 1) for x in parts], axis=1
            )

        def proj_whole(layer):
            return (proj_0, proj_1)[layer]

        def in_whole(layer):
            zeros = jnp.zeros((width, hidden), BF)
            part = (fc_0, fc_1)[layer][0]
            return lax.dynamic_update_slice_in_dim(zeros, part, member * hid, 1)

        def out_whole(layer):
            zeros = jnp.zeros((hidden, width), BF)
            part = (fc_0, fc_1)[layer][1]
            return lax.dynamic_update_slice_in_dim(zeros, part, member * hid, 0)

        attn_sum = summed(attn_whole, edge)
        proj_sum = summed(proj_whole, attn_sum)
        in_sum = summed(in_whole, proj_sum)
        out_sum = summed(out_whole, in_sum)
        small = pick(small_0, small_1) + cross(pick(small_1, small_0))
        small = lax.psum(small, chip_axes)
    return (
        edge,
        attn_sum[None],
        proj_sum[None],
        in_sum[None],
        out_sum[None],
        small[: 2 * width].reshape(1, 2, width),
        small[2 * width : 8 * width].reshape(1, 6, width),
        small[8 * width :][None],
    )


def solution(mesh):
    sections, replicas, shards = (mesh.shape[name] for name in ("section", "replica", "shard"))
    split = Mesh(
        mesh.devices.reshape(sections, replicas, replicas, shards // replicas),
        ("section", "replica", "seq", "sub"),
    )
    rows = ("seq", "sub")
    return jax.shard_map(
        partial(body, replicas, shards),
        mesh=split,
        in_specs=(
            P("section", None, "replica", rows, None),
            P(None, "replica", None),
            P("section", rows, None),
            P("section", rows, None),
            P("section", rows, None),
            P("section", rows, None),
            P("section", None, None),
            P("section", None, None),
            P("section", None),
        ),
        out_specs=(
            P("section", None, "replica", rows, None),
            P("section", rows, None),
            P("section", rows, None),
            P("section", rows, None),
            P("section", rows, None),
            P("section", None, None),
            P("section", None, None),
            P("section", None),
        ),
        check_vma=False,
    )
```

```python
from functools import partial

import jax
import jax.numpy as jnp
from jax import lax
from jax.experimental import pallas as pl
from jax.experimental.pallas import tpu as pltpu
from jax.sharding import Mesh, PartitionSpec as P

HEADS = 25
HEAD = 64
EPSILON = 1e-05
MASKED = -1e30
BF = jnp.bfloat16
F32 = jnp.float32
SWAP = [(0, 1), (1, 0)]
SIDE = [(0, 1), (1, 0), (2, 3), (3, 2)]
ACROSS = [(0, 2), (2, 0), (1, 3), (3, 1)]
CORNER = [(0, 3), (3, 0), (1, 2), (2, 1)]


def dot(left, right, contract):
    return lax.dot_general(
        left, right, ((contract[:1], contract[1:]), ((), ())), preferred_element_type=F32
    )


def norm_stats(value, mask, width):
    mean = jnp.sum(value, axis=-1, keepdims=True) * (1.0 / width)
    centred = value - mean if mask is None else (value - mean) * mask
    variance = jnp.sum(centred * centred, axis=-1, keepdims=True) * (1.0 / width)
    inverse = lax.rsqrt(variance + EPSILON)
    return centred * inverse, inverse


def norm_back(grad, value, gain, mask, width):
    unit, inverse = norm_stats(value, mask, width)
    grad_unit = grad * gain
    mean_one = jnp.sum(grad_unit, axis=-1, keepdims=True) * (1.0 / width)
    mean_two = jnp.sum(grad_unit * unit, axis=-1, keepdims=True) * (1.0 / width)
    grad_value = inverse * (grad_unit - mean_one - unit * mean_two)
    if mask is not None:
        grad_value = grad_value * mask
    return grad_value, jnp.sum(grad * unit, axis=0), jnp.sum(grad, axis=0)


def gelu_pair(x):
    c = 0.7978845608028654
    square = x * x
    th = jnp.tanh(c * x * (1.0 + 0.044715 * square))
    value = 0.5 * x * (1.0 + th)
    slope = 0.5 * (1.0 + th) + 0.5 * x * (1.0 - th * th) * c * (1.0 + 3 * 0.044715 * square)
    return value, slope


def spots(chunk, piece, block, n, teams):
    order = ((0, 2, 1, 3), (0, 1, 2, 3))[chunk]
    return [
        (index * n, order[piece * (block // n) + index], chunk * n) for index in range(block // n)
    ]


def attend_kernel(grouped, q_ref, k_ref, v_ref, bias_ref, *out_refs):
    *outs, lse_ref = out_refs
    length = q_ref.shape[1]
    half = length // 2
    n = half // 4
    block = min(256, half)
    for chunk in range(2):
        extent = half * (chunk + 1)
        for piece in range(half // block):
            at = chunk * half + piece * block
            query = q_ref[:, at : at + block] * jnp.asarray(HEAD ** (-0.5), BF)
            scores = dot(k_ref[:, :extent], query, (0, 0)) + bias_ref[:extent, at : at + block]
            best = jnp.max(scores, axis=0, keepdims=True)
            weights = jnp.exp(scores - best)
            total = jnp.sum(weights, axis=0, keepdims=True)
            out = dot(v_ref[:, :extent], weights.astype(BF), (1, 0)) / total
            out = out.astype(BF)
            if grouped:
                for here, owner, there in spots(chunk, piece, block, n, 4):
                    outs[owner][:, there : there + n] = out[:, here : here + n]
            else:
                outs[0][:, at : at + block] = out
            lse_ref[0, :, at : at + block] = best + jnp.log(total)


def attend_back_kernel(grouped, q_ref, k_ref, v_ref, bias_ref, lse_ref, *refs):
    *g_refs, out_ref, keys, values = refs
    head = pl.program_id(0)
    slots = pl.num_programs(0)
    length = q_ref.shape[1]
    half = length // 2
    n = half // 4
    block = min(256, half)
    scale = HEAD ** (-0.5)
    keys[...] = jnp.zeros_like(keys)
    values[...] = jnp.zeros_like(values)
    for chunk in range(2):
        extent = half * (chunk + 1)
        for piece in range(half // block):
            at = chunk * half + piece * block
            query = q_ref[:, at : at + block] * jnp.asarray(scale, BF)
            if grouped:
                grad = jnp.concatenate(
                    [
                        g_refs[owner][:, there : there + n]
                        for _, owner, there in spots(chunk, piece, block, n, 4)
                    ],
                    axis=1,
                )
            else:
                grad = g_refs[0][:, at : at + block]
            scores = dot(k_ref[:, :extent], query, (0, 0)) + bias_ref[:extent, at : at + block]
            probs = jnp.exp(scores - lse_ref[0, :, at : at + block])
            inner = dot(v_ref[:, :extent], grad, (0, 0))
            rowdot = jnp.sum(probs * inner, axis=0, keepdims=True)
            dscore = (probs * (inner - rowdot)).astype(BF)
            values[:, :extent] += dot(grad, probs.astype(BF), (1, 1))
            keys[:, :extent] += dot(query, dscore, (1, 1))
            grad_query = (dot(k_ref[:, :extent], dscore, (1, 0)) * scale).astype(BF)
            out_ref[pl.ds(pl.multiple_of(head * HEAD, HEAD), HEAD), at : at + block] = grad_query
    key_rows = pl.ds(pl.multiple_of((slots + head) * HEAD, HEAD), HEAD)
    value_rows = pl.ds(pl.multiple_of((2 * slots + head) * HEAD, HEAD), HEAD)
    out_ref[key_rows, :] = keys[...].astype(BF)
    out_ref[value_rows, :] = values[...].astype(BF)

    @pl.when(head == 0)
    def _():
        used = 3 * HEAD * pl.num_programs(0)
        spare = out_ref.shape[0] % (3 * HEAD)
        if spare:
            rest = pl.ds(pl.multiple_of(used, HEAD), spare)
            out_ref[rest, :] = jnp.zeros((spare, length), BF)


def attend(mixed, bias, slots, grouped):
    length = mixed.shape[1]
    part = lambda first: pl.BlockSpec((HEAD, length), lambda h: (first + h, 0))
    whole = pl.BlockSpec((length, length), lambda h: (0, 0))
    count, span = (4, length // 4) if grouped else (1, length)
    *outs, lse = pl.pallas_call(
        partial(attend_kernel, grouped),
        grid=(slots,),
        in_specs=[part(0), part(slots), part(2 * slots), whole],
        out_specs=[pl.BlockSpec((HEAD, span), lambda h: (h, 0))] * count
        + [pl.BlockSpec((1, 1, length), lambda h: (h, 0, 0))],
        out_shape=[jax.ShapeDtypeStruct((slots * HEAD, span), BF)] * count
        + [jax.ShapeDtypeStruct((slots, 1, length), F32)],
        compiler_params=pltpu.CompilerParams(vmem_limit_bytes=40 * 2**20),
        cost_estimate=pl.CostEstimate(
            flops=42 * slots * length * length * HEAD,
            bytes_accessed=4 * length * length + 8 * slots * HEAD * length,
            transcendentals=slots * length * length,
        ),
    )(mixed, mixed, mixed, bias)
    return outs, lse


def attend_back(mixed, grads, bias, lse, slots, grouped):
    length = mixed.shape[1]
    part = lambda first: pl.BlockSpec((HEAD, length), lambda h: (first + h, 0))
    whole = pl.BlockSpec((length, length), lambda h: (0, 0))
    count, span = (4, length // 4) if grouped else (1, length)
    return pl.pallas_call(
        partial(attend_back_kernel, grouped),
        grid=(slots,),
        in_specs=[
            part(0),
            part(slots),
            part(2 * slots),
            whole,
            pl.BlockSpec((1, 1, length), lambda h: (h, 0, 0)),
        ]
        + [pl.BlockSpec((HEAD, span), lambda h: (h, 0))] * count,
        out_specs=pl.BlockSpec(mixed.shape, lambda h: (0, 0)),
        out_shape=jax.ShapeDtypeStruct(mixed.shape, BF),
        scratch_shapes=[pltpu.VMEM((HEAD, length), F32), pltpu.VMEM((HEAD, length), F32)],
        compiler_params=pltpu.CompilerParams(vmem_limit_bytes=40 * 2**20),
        cost_estimate=pl.CostEstimate(
            flops=48 * slots * length * length * HEAD,
            bytes_accessed=4 * length * length + 14 * slots * HEAD * length,
            transcendentals=slots * length * length,
        ),
    )(mixed, mixed, mixed, bias, lse, *grads)


TOPS = (0, 2, 1, 3)
LOWS = (0, 1, 2, 3)


def kernel_call(kernel, member, inputs, outputs, scratch=()):
    count = len(inputs)
    size = sum(x.size * x.dtype.itemsize for x in inputs)
    size += sum(x.size * x.dtype.itemsize for x in outputs)
    return pl.pallas_call(
        kernel,
        in_specs=[pl.BlockSpec(memory_space=pltpu.SMEM)]
        + [pl.BlockSpec(memory_space=pltpu.VMEM)] * count,
        out_specs=[pl.BlockSpec(memory_space=pltpu.VMEM)] * len(outputs),
        out_shape=outputs,
        scratch_shapes=list(scratch),
        compiler_params=pltpu.CompilerParams(vmem_limit_bytes=48 * 2**20),
        cost_estimate=pl.CostEstimate(flops=0, bytes_accessed=size, transcendentals=0),
    )(member.reshape(1), *inputs)


def chosen_kernel(kernel, count, section_ref, *refs):
    inputs, out_ref = refs[: 2 * count], refs[2 * count]
    held, sem = refs[2 * count + 1 : -1], refs[-1]
    for side in range(2):

        @pl.when(section_ref[0] == side)
        def _(side=side):
            copies = [
                pltpu.make_async_copy(inputs[2 * i + side], held[i], sem.at[i])
                for i in range(count)
            ]
            for copy in copies:
                copy.start()
            for copy in copies:
                copy.wait()

    kernel(section_ref, *held, out_ref)


def chosen_call(kernel, section, pairs, out):
    count = len(pairs)
    size = sum(a.size * a.dtype.itemsize for a, _ in pairs) + out.size * out.dtype.itemsize
    return pl.pallas_call(
        partial(chosen_kernel, kernel, count),
        in_specs=[pl.BlockSpec(memory_space=pltpu.SMEM)]
        + [pl.BlockSpec(memory_space=pl.ANY)] * (2 * count),
        out_specs=pl.BlockSpec(memory_space=pltpu.VMEM),
        out_shape=out,
        scratch_shapes=[pltpu.VMEM(a.shape, a.dtype) for a, _ in pairs]
        + [pltpu.SemaphoreType.DMA((count,))],
        compiler_params=pltpu.CompilerParams(vmem_limit_bytes=48 * 2**20),
        cost_estimate=pl.CostEstimate(flops=0, bytes_accessed=size, transcendentals=0),
    )(section.reshape(1), *[x for pair in pairs for x in pair])


def slab_places(member, rows, step, slab):
    found = []
    for part, order in enumerate((TOPS, LOWS)):
        for turn in order:
            owner = member ^ turn
            for block in (2 * part, 2 * part + 1):
                found.append((owner, block * rows + owner * step))
    return found


def sort_heads_kernel(slots, rows, step, slab, member_ref, *refs):
    *got, out_ref, whole = refs
    member = member_ref[0]
    width = whole.shape[0]
    high = slots * HEAD
    for turn in range(4):
        owner = member ^ turn
        at = jnp.minimum(owner * high, width - high)
        spare = (owner * high - at) // HEAD
        if turn == 0:
            pass
        for slot in range(slots):

            @pl.when(slot >= spare)
            def _(turn=turn, slot=slot, at=at):
                to = pl.multiple_of(at + slot * HEAD, HEAD)
                whole[pl.ds(to, HEAD), :] = got[turn][slot * HEAD : (slot + 1) * HEAD, :]

    line = lax.broadcasted_iota(jnp.int32, (slab, 1), 0)
    for index, (owner, at) in enumerate(slab_places(member, rows, step, slab)):
        rows_here = whole[pl.ds(pl.multiple_of(at, 16), slab), :]
        keep = (line < step) | (owner == 3)
        out_ref[index * slab : (index + 1) * slab, :] = jnp.where(
            keep, rows_here, jnp.zeros_like(rows_here)
        )


def split_heads_kernel(slots, rows, step, slab, member_ref, value_ref, *refs):
    *outs, whole = refs
    member = member_ref[0]
    width = whole.shape[0]
    high = slots * HEAD
    for index, (owner, at) in enumerate(slab_places(member, rows, step, slab)):
        first = index * slab
        whole[pl.ds(pl.multiple_of(at, 16), step), :] = value_ref[first : first + step, :]

        @pl.when(owner == 3)
        def _(first=first, at=at):
            to = pl.multiple_of(at + step, 16)
            whole[pl.ds(to, slab - step), :] = value_ref[first + step : first + slab, :]

    for turn in range(4):
        owner = member ^ turn
        at = jnp.minimum(owner * high, width - high)
        spare = owner * high - at
        line = lax.broadcasted_iota(jnp.int32, (high, 1), 0)
        rows_here = whole[pl.ds(pl.multiple_of(at, HEAD), high), :]
        outs[turn][...] = jnp.where(line >= spare, rows_here, jnp.zeros_like(rows_here))


def member_rows(refs, member, owner, cut, rows):
    if member is None:
        at = owner * rows
        return [
            (ref[at : at + cut, :].astype(F32), ref[at + cut : at + rows, :].astype(F32))
            for ref in refs
        ]
    turn = member ^ owner
    twin = (turn & 1) * 2 + turn // 2
    found = []
    for ref in refs:
        top = ref[pl.ds(pl.multiple_of(twin * cut, 16), cut), :]
        low = ref[pl.ds(pl.multiple_of(4 * cut + turn * (rows - cut), 16), rows - cut), :]
        found.append((top.astype(F32), low.astype(F32)))
    return found


def blocks_into(out_ref, lines, value, block, padded):
    for index in range(value.shape[1] // padded):
        out_ref[lines, index * block : (index + 1) * block] = value[
            :, index * padded : index * padded + block
        ]


def finish_attn_kernel(slots, cut, total, _, left_ref, right_ref, out_ref):
    member = None
    rows = out_ref.shape[0]
    width = out_ref.shape[1] // 3
    high = slots * HEAD
    held = left_ref.shape[0] // 4
    for owner in range(4):
        start = min(owner * high, width - high)
        spare = owner * high - start
        (left, right) = member_rows((left_ref, right_ref), member, owner, cut, held)
        for lines, first, size in ((0, 0, cut), (1, cut, rows - cut)):
            shared = left[lines].shape[1] * 2 - total
            both = jnp.concatenate([left[lines], right[lines][:, shared:]], axis=1)
            for third in range(3):
                to = third * width + start + spare
                out_ref[first : first + size, to : to + high - spare] = both[
                    :size, third * high + spare : (third + 1) * high
                ]


def finish_proj_kernel(step, slab, cut, total, padded, _, left_ref, right_ref, out_ref):
    member = None
    block = out_ref.shape[1] // 4
    for owner in range(4):
        size = slab if owner == 3 else step
        (left, right) = member_rows((left_ref, right_ref), member, owner, cut, slab)
        for lines, first, count in ((0, 0, cut), (1, cut, size - cut)):
            shared = left[lines].shape[1] * 2 - total
            both = jnp.concatenate([left[lines], right[lines][:, shared:]], axis=1)[:count]
            at = owner * step + first
            blocks_into(out_ref, slice(at, at + count), both, block, padded)


def finish_in_kernel(cut, padded, _, value_ref, out_ref):
    member = None
    rows = out_ref.shape[0]
    part = out_ref.shape[1] // 16
    for owner in range(4):
        ((top, low),) = member_rows((value_ref,), member, owner, cut, padded)
        for block in range(4):
            to = (block * 4 + owner) * part
            out_ref[:cut, to : to + part] = top[:, block * padded : block * padded + part]
            out_ref[cut:, to : to + part] = low[
                : rows - cut, block * padded : block * padded + part
            ]


def finish_out_kernel(cut, padded, _, value_ref, out_ref):
    member = None
    rows = out_ref.shape[0] // 4
    block = out_ref.shape[1] // 4
    for owner in range(4):
        ((top, low),) = member_rows((value_ref,), member, owner, cut, padded)
        at = owner * rows
        blocks_into(out_ref, slice(at, at + cut), top, block, padded)
        blocks_into(out_ref, slice(at + cut, at + rows), low[: rows - cut], block, padded)


def expand_kernel(padded, _, *refs):
    half = len(refs) // 2
    for value_ref, out_ref in zip(refs[:half], refs[half:]):
        block = value_ref.shape[1] // 4
        out_ref[...] = jnp.zeros_like(out_ref)
        for index in range(4):
            out_ref[:, index * padded : index * padded + block] = value_ref[
                :, index * block : (index + 1) * block
            ]


def edge_kernel(padded, section_ref, mine_ref, other_ref, edge_ref):
    block = edge_ref.shape[4] // 4
    wide = 4 * padded
    for side, refs in enumerate(((mine_ref, other_ref), (other_ref, mine_ref))):

        @pl.when(section_ref[0] == side)
        def _(side=side, refs=refs):
            for index, ref in enumerate(refs):
                value = ref[:, side * wide : (side + 1) * wide].astype(F32)
                blocks_into(edge_ref.at[0, index, 0], slice(None), value, block, padded)


def order_kernel(forth, place_ref, value_ref, out_ref):
    n = value_ref.shape[0] // 8
    at = 0
    for part, order in enumerate((TOPS, LOWS)):
        for turn in order:
            rows = pl.ds(pl.multiple_of(((place_ref[0] ^ turn) * 2 + part) * n, n), n)
            if forth:
                out_ref[at : at + n, :] = value_ref[rows, :]
            else:
                out_ref[rows, :] = value_ref[at : at + n, :]
            at += n


def deal_kernel(whole_in, whole_out, places_ref, *refs):
    place = places_ref[0]
    count = 1 if whole_in else 4
    inputs, outs = refs[:count], refs[count:]
    size = inputs[0].shape[0] // (4 if whole_in else 1)
    for turn in range(4):
        at = pl.multiple_of((place ^ turn) * size, size)
        if whole_in:
            outs[turn][...] = inputs[0][pl.ds(at, size), :]
        elif whole_out:
            outs[0][pl.ds(at, size), :] = inputs[turn][...]
        else:
            for owner in range(4):

                @pl.when((place ^ turn) == owner)
                def _(turn=turn, owner=owner):
                    outs[turn][...] = inputs[owner][...]


def join_kernel(_, own, near_a, near_b, far_a, far_b, *out_refs):
    n, m = near_a.shape[0], near_b.shape[0]
    at = 0
    for part, first, size in (
        (own, 0, n),
        (near_a, 0, n),
        (far_a, 0, 2 * n),
        (own, n, m),
        (near_b, 0, m),
        (far_b, 0, 2 * m),
    ):
        column = 0
        for out_ref in out_refs:
            width = out_ref.shape[1]
            out_ref[at : at + size, :] = part[first : first + size, column : column + width]
            column += width
        at += size


def place_kernel(widths, member_ref, *refs):
    pieces, outs = refs[:4], refs[4:]
    rows = pieces[0].shape[0]
    for turn in range(4):
        at = pl.multiple_of((member_ref[0] ^ turn) * rows, 16)
        column = 0
        for width, out_ref in zip(widths, outs):
            out_ref[pl.ds(at, rows), :] = pieces[turn][:, column : column + width]
            column += width


def total_kernel(place_ref, *refs):
    pieces, out_ref = refs[:4], refs[4]
    for place in range(4):

        @pl.when(place_ref[0] == place)
        def _(place=place):
            first, second, third, fourth = (pieces[place ^ turn][...] for turn in range(4))
            out_ref[...] = ((first + second) + third) + fourth


def same_kernel(*refs):
    pass


def tie(value, *others):
    any_place = pl.BlockSpec(memory_space=pl.ANY)
    return pl.pallas_call(
        same_kernel,
        in_specs=[any_place] * (1 + len(others)),
        out_specs=any_place,
        out_shape=jax.ShapeDtypeStruct(value.shape, value.dtype),
        input_output_aliases={0: 0},
        cost_estimate=pl.CostEstimate(flops=0, bytes_accessed=0, transcendentals=0),
    )(value, *others)


def body(
    replicas,
    shards,
    boundary,
    segments,
    attn_weight,
    proj_weight,
    fc_in_weight,
    fc_out_weight,
    norm_gains,
    vector_bias,
    fc_in_bias,
):
    sub = shards // replicas
    team = replicas * sub
    fast = replicas == 4 and sub == 1
    team_axes = ("replica", "sub")
    row_axes = ("seq", "sub")
    chip_axes = ("replica", "seq", "sub")
    section = lax.axis_index("section")
    first = section == 0
    member = lax.axis_index(team_axes)
    local = boundary.shape[3]
    width = boundary.shape[4]
    hidden = fc_in_bias.shape[1]
    n = local // 2
    length = segments.shape[2]
    half = length // 2
    slots = -(-HEADS // team)
    heads_width = slots * HEAD
    hid = hidden // team
    block = width // 4
    padded = -(-block // 32) * 32 if fast else block
    wide = 4 * padded
    mask = None
    if fast:
        mask = (jnp.arange(wide) % padded < block).astype(F32)
    mixed_rows = -(-3 * heads_width // 128) * 128 if fast else 3 * heads_width
    attn_half = -(-mixed_rows // 256) * 128
    proj_half = -(-wide // 256) * 128

    def head_start(index):
        return jnp.minimum(index * slots, HEADS - slots)

    def spare_heads(index):
        return min(max(index * slots - (HEADS - slots), 0), slots)

    start = head_start(member) * HEAD

    def cross(value, pairs=SWAP):
        return lax.ppermute(value, "section", pairs)

    def side(value):
        return lax.ppermute(value, "replica", SIDE)

    def across(value):
        return lax.ppermute(value, "replica", ACROSS)

    def corner(value):
        return lax.ppermute(value, "replica", CORNER)

    def pick(a, b):
        return jnp.where(first, a, b)

    def halves(value, half, axis):
        size = value.shape[axis]
        left = lax.slice_in_dim(value, 0, half, axis=axis)
        right = lax.slice_in_dim(value, size - half, size, axis=axis)
        return pick(left, right), pick(right, left)

    def spaced(vector):
        if not fast:
            return vector
        parts = vector.reshape(-1, 4, block)
        parts = jnp.pad(parts, ((0, 0), (0, 0), (0, padded - block)))
        return parts.reshape(vector.shape[:-1] + (wide,))

    def dense(vector):
        if not fast:
            return vector
        return vector.reshape(vector.shape[:-1] + (4, padded))[..., :block].reshape(
            vector.shape[:-1] + (width,)
        )

    def flat(p, z):
        return p * shards + z

    rounds = []
    for turn in range(2):
        pairs = []
        for p in range(replicas):
            for z in range(shards):
                slot = z // (shards // 2)
                h = turn if slot == 0 else 1 - turn
                j = 2 * (z % (shards // 2)) + h
                target = flat(j // sub, p * sub + j % sub)
                pairs.append((flat(p, z), target))
        rounds.append(pairs)
    place = lax.axis_index(row_axes)
    early = place < shards // 2
    even = member % 2 == 0

    def to_team_far(value):
        top, low = value[:n], value[n:]
        one = lax.ppermute(jnp.where(early, top, low), chip_axes, rounds[0])
        two = lax.ppermute(jnp.where(early, low, top), chip_axes, rounds[1])
        return jnp.concatenate([jnp.where(even, one, two), jnp.where(even, two, one)])

    def from_team_far(value):
        top, low = value[:n], value[n:]
        one = lax.ppermute(
            jnp.where(even, top, low), chip_axes, [(b, a) for a, b in rounds[0]]
        )
        two = lax.ppermute(
            jnp.where(even, low, top), chip_axes, [(b, a) for a, b in rounds[1]]
        )
        return jnp.concatenate([jnp.where(early, one, two), jnp.where(early, two, one)])

    plane = lax.axis_index("seq")

    def turned(pieces, axis):
        own, *others = pieces
        return [own] + [
            lax.ppermute(x, axis, pairs) for x, pairs in zip(others, (SIDE, ACROSS, CORNER))
        ]

    def dealt(place, pieces, whole_in, whole_out):
        rows, columns = pieces[0].shape
        if whole_in:
            outs = [jax.ShapeDtypeStruct((rows // 4, columns), BF)] * 4
        elif whole_out:
            outs = [jax.ShapeDtypeStruct((rows * 4, columns), BF)]
        else:
            outs = [jax.ShapeDtypeStruct((rows, columns), BF)] * 4
        return kernel_call(partial(deal_kernel, whole_in, whole_out), place, pieces, outs)

    def to_team(value):
        if not fast:
            return to_team_far(value)
        pieces = turned(dealt(member, [value], True, False), "replica")
        pieces = turned(dealt(plane ^ member, pieces, False, False), "seq")
        return dealt(plane, pieces, False, True)[0]

    def from_team(value):
        if not fast:
            return from_team_far(value)
        pieces = turned(dealt(plane, [value], True, False), "seq")
        pieces = turned(dealt(plane ^ member, pieces, False, False), "replica")
        return dealt(member, pieces, False, True)[0]

    if fast:
        order_a = [member, member ^ 2, member ^ 1, member ^ 3]
        order_b = [member, member ^ 1, member ^ 2, member ^ 3]
    else:
        order_a = order_b = list(range(team))

    def gather_near(value, cut, widths=None):
        a, b = value[:cut], value[cut:]
        if not fast:
            whole = jnp.concatenate(
                [
                    lax.all_gather(a, team_axes, axis=0, tiled=True),
                    lax.all_gather(b, team_axes, axis=0, tiled=True),
                ]
            )
            return whole, whole
        near_a, near_b = across(a), side(b)
        return gather_far(value, cut, near_a, near_b, widths), near_b

    def gather_far(value, cut, near_a, near_b, widths=None):
        a, b = value[:cut], value[cut:]
        far_a = side(jnp.concatenate([a, near_a]))
        far_b = across(jnp.concatenate([b, near_b]))
        outs = [
            jax.ShapeDtypeStruct((4 * value.shape[0], width), value.dtype)
            for width in widths or [value.shape[1]]
        ]
        parts = [value, near_a, near_b, far_a, far_b]
        outs = kernel_call(join_kernel, member, parts, outs)
        return outs if widths else outs[0]

    def gather(value, cut):
        return gather_near(value, cut)[0]

    def gather_many(values, cut):
        whole = jnp.concatenate(values, axis=1)
        return gather_near(whole, cut, [value.shape[1] for value in values])[0]

    def gather_direct(value, widths=None):
        pieces = [value, side(value), across(value), corner(value)]
        widths = widths or [value.shape[1]]
        rows = 4 * value.shape[0]
        outs = [jax.ShapeDtypeStruct((rows, width), value.dtype) for width in widths]
        return kernel_call(partial(place_kernel, widths), member, pieces, outs)

    def edge_of(value):
        return lax.slice(value, (0, 0), (16, 128))

    def ordered(forth, value):
        out = jax.ShapeDtypeStruct(value.shape, value.dtype)
        return kernel_call(partial(order_kernel, forth), member, [value], [out])[0]

    def gather_late(value):
        if not fast:
            return gather(value, n)
        whole = lax.all_gather(value, "replica", axis=0, tiled=True)
        return ordered(True, whole)

    def scatter_late(value):
        if not fast:
            return scatter(value)
        whole = ordered(False, value)
        return lax.psum_scatter(whole, "replica", scatter_dimension=0, tiled=True)


    def scatter(value, got=None):
        middle_row = value.shape[0] // 2
        a, b = value[:middle_row], value[middle_row:]
        if not fast:
            return jnp.concatenate(
                [
                    lax.psum_scatter(a.astype(F32), team_axes, scatter_dimension=0, tiled=True),
                    lax.psum_scatter(b.astype(F32), team_axes, scatter_dimension=0, tiled=True),
                ]
            )
        m = middle_row // 4
        got_a, got_b = got or scatter_first(value)
        sent_a = (a[m : 2 * m].astype(F32) + got_a[m:]).astype(BF)
        sent_b = (b[m : 2 * m].astype(F32) + got_b[m:]).astype(BF)
        last_a, last_b = across(sent_a), side(sent_b)
        sum_a = a[:m].astype(F32) + got_a[:m] + last_a
        sum_b = b[:m].astype(F32) + got_b[:m] + last_b
        return jnp.concatenate([sum_a, sum_b])

    def scatter_first(value):
        middle_row = value.shape[0] // 2
        m = middle_row // 4
        return side(value[2 * m : middle_row]), across(value[middle_row + 2 * m :])

    if fast:
        rows = width // replicas
        slab = -(-rows // 64) * 16
        step = (rows - slab) // 3
        cut = padded // 2
        sorted_heads = jax.ShapeDtypeStruct((16 * slab, 2 * n), BF)
        one = jax.ShapeDtypeStruct((heads_width, 2 * n), BF)
        scratch = [pltpu.VMEM((width, 2 * n), BF)]

    def heads_to_tokens(values):
        if fast:
            own, near, over, far = values
            got = [own, side(near), across(over), corner(far)]
            kernel = partial(sort_heads_kernel, slots, rows, step, slab)
            return kernel_call(kernel, member, got, [sorted_heads], scratch)[0]
        pieces = values[0].reshape(heads_width, 2, team, n).transpose(2, 0, 1, 3)
        got = lax.all_to_all(pieces, team_axes, 0, 0, tiled=True)
        got = got.reshape(team, heads_width, 2 * n)
        pieces = []
        for index in range(team):
            spare = spare_heads(index) * HEAD
            if spare < heads_width:
                pieces.append(got[index, spare:])
        return jnp.concatenate(pieces)

    def tokens_to_heads(value):
        if fast:
            kernel = partial(split_heads_kernel, slots, rows, step, slab)
            own, near, over, far = kernel_call(kernel, member, [value], [one] * 4, scratch)
            return [own, side(near), across(over), corner(far)]

        def of(index):
            return lax.dynamic_slice_in_dim(value, head_start(index) * HEAD, heads_width, 0)

        pieces = jnp.stack([of(index) for index in range(team)])
        got = lax.all_to_all(pieces, team_axes, 0, 0, tiled=True)
        got = got.reshape(team, heads_width, 2, n).transpose(1, 2, 0, 3)
        whole = got.reshape(heads_width, length)
        spare = member * slots - head_start(member)
        lines = lax.broadcasted_iota(jnp.int32, (heads_width, 1), 0)
        return [jnp.where(lines >= spare * HEAD, whole, jnp.zeros_like(whole))]

    def head_columns(weight):
        return [
            lax.dynamic_slice_in_dim(weight, third * width + start, heads_width, 1)
            for third in range(3)
        ]

    if fast:
        hid_part = hid // replicas
        more = padded - rows
        own_attn = jnp.concatenate(head_columns(attn_weight[0]), axis=1)
        own_attn = jnp.pad(own_attn, ((0, more), (0, mixed_rows - 3 * heads_width)))
        own_in = jnp.concatenate(
            [
                jnp.pad(
                    lax.dynamic_slice_in_dim(
                        fc_in_weight[0], part * hid + member * hid_part, hid_part, 1
                    ),
                    ((0, more), (0, padded - hid_part)),
                )
                for part in range(replicas)
            ],
            axis=1,
        )
        own_out = lax.dynamic_slice_in_dim(fc_out_weight[0], member * hid_part, hid_part, 0)
        own_proj = lax.dynamic_slice_in_dim(proj_weight[0], member * step, slab, 0)
        own_out, own_proj = kernel_call(
            partial(expand_kernel, padded),
            member,
            [own_out, own_proj],
            [jax.ShapeDtypeStruct((hid_part, wide), BF), jax.ShapeDtypeStruct((slab, wide), BF)],
        )
        own_out = jnp.pad(own_out, ((0, padded - hid_part), (0, 0)))

        def gathered(piece):
            return lax.all_gather(piece, "seq", axis=0, tiled=True)

        def full(mine):
            other = cross(mine)
            return pick(mine, other), pick(other, mine)

        def spread(pair):
            got = cross(pair[1])
            return pick(pair[0], got), pick(got, pair[0])

        attn_pieces = spread(halves(own_attn, attn_half, 1))
        fc_pieces = spread((pick(own_in, own_out), pick(own_out, own_in)))
        shared = 2 * attn_half - mixed_rows
        attn_got = [gathered(attn_pieces[0])]
        proj_got = []
        fc_got = []
        proj_whole = []

        def fetch_proj(after):
            proj_got.append(gathered(tie(own_proj, after)))

        def fetch_fc(layer, after):
            fc_got.append(gathered(tie(fc_pieces[layer], after)))

        def fetch_attn(after):
            attn_got.append(gathered(tie(attn_pieces[1], after)))

        def get_attn(layer, after):
            left, right = full(tie(attn_got[layer], after))
            return jnp.concatenate([left, right[:, shared:]], axis=1)

        def get_proj(layer, near=None, after=None):
            if layer == 0:
                mine = tie(proj_got[0], near)
                near = across(mine[: 2 * slab]), side(mine[2 * slab :])
                near = [tie(value, after) for value in near]
                mine = gather_far(mine, 2 * slab, *near)
                other = cross(mine)
                proj_whole.extend([pick(mine, other), pick(other, mine)])
            return proj_whole[layer]

        def get_fc(layer, after):
            return full(tie(fc_got[layer], after))

        def hid_of(vector):
            mine = lax.dynamic_slice_in_dim(
                vector.reshape(replicas, replicas, hid_part), member, 1, 1
            )
            return jnp.pad(mine[:, 0], ((0, 0), (0, padded - hid_part))).reshape(wide)

        def hid_into(vector):
            zeros = jnp.zeros((replicas, replicas, hid_part), F32)
            return lax.dynamic_update_slice_in_dim(
                zeros, vector.reshape(replicas, 1, padded)[..., :hid_part], member, 1
            ).reshape(hidden)

    else:

        def both(value):
            other = cross(value)
            return pick(value, other), pick(other, value)

        def weights_of(layer):
            def whole(weight):
                return lax.all_gather(both(weight[0])[layer], row_axes, axis=0, tiled=True)

            w_attn = jnp.concatenate(head_columns(whole(attn_weight)), axis=1)
            w_proj = whole(proj_weight)
            w_in = lax.dynamic_slice_in_dim(whole(fc_in_weight), member * hid, hid, 1)
            w_out = lax.dynamic_slice_in_dim(whole(fc_out_weight), member * hid, hid, 0)
            return w_attn, w_proj, w_in, w_out

        whole_weights = [weights_of(0), weights_of(1)]

        def fetch_proj(after):
            pass

        def fetch_fc(layer, after):
            pass

        fetch_attn = fetch_proj

        def get_attn(layer, after):
            return whole_weights[layer][0]

        def get_proj(layer, *others):
            return whole_weights[layer][1]

        def get_fc(layer, after):
            return whole_weights[layer][2:]

        def hid_of(vector):
            return lax.dynamic_slice_in_dim(vector, member * hid, hid, 0)

        def hid_into(vector):
            return lax.dynamic_update_slice_in_dim(
                jnp.zeros((hidden,), F32), vector, member * hid, 0
            )

    def heads_into(vector):
        return lax.dynamic_update_slice_in_dim(jnp.zeros((width,), F32), vector, start, 0)

    block_0, block_1 = boundary[0, 0, 0], boundary[0, 1, 0]
    if fast:
        block_0, block_1 = kernel_call(
            partial(expand_kernel, padded),
            member,
            [block_0, block_1],
            [jax.ShapeDtypeStruct((local, wide), BF)] * 2,
        )
    kept = pick(block_0, block_1)
    got = cross(pick(block_1, block_0))
    source = to_team(pick(kept, got))
    cotangent = pick(got, kept)
    vectors = jnp.concatenate([norm_gains[0].ravel(), vector_bias[0].ravel(), fc_in_bias[0]])
    other_vectors = cross(vectors)
    vectors = (pick(vectors, other_vectors), pick(other_vectors, vectors))

    ids = lax.dynamic_index_in_dim(segments, section, 0, keepdims=False)[0]
    swapped = [
        (flat(p, z * sub + k), flat(z, p * sub + k))
        for p in range(replicas)
        for z in range(replicas)
        for k in range(sub)
    ]
    ids = lax.ppermute(ids, chip_axes, swapped).reshape(2, team, n)
    places, names = [], []
    for chunk, order in enumerate((order_a, order_b)):
        for index in order:
            places.append(chunk * half + index * n + jnp.arange(n, dtype=jnp.int32))
            names.append(lax.dynamic_index_in_dim(ids[chunk], index, 0, keepdims=False))
    if fast:
        places, names = [], []
        ids = ids.reshape(2, 2, team, n // 2)
        for chunk, order in enumerate((order_a, order_b)):
            for index in order:
                for part in range(2):
                    at = chunk * half + part * (half // 2) + index * (n // 2)
                    places.append(at + jnp.arange(n // 2, dtype=jnp.int32))
                    names.append(
                        lax.dynamic_index_in_dim(ids[chunk, part], index, 0, keepdims=False)
                    )
    places, names = jnp.concatenate(places), jnp.concatenate(names)
    allowed = (names[:, None] == names[None, :]) & (places[:, None] <= places[None, :])
    bias = jnp.where(allowed, 0.0, MASKED).astype(F32)

    def parameters(layer):
        vector = vectors[layer]
        lines = vector[: 8 * width].reshape(8, width)
        query_bias = lax.dynamic_slice_in_dim(lines[3], start, heads_width, 0)
        value_bias = lax.dynamic_slice_in_dim(lines[4], start, heads_width, 0)
        lines = spaced(lines)
        gains, biases = lines[:2], lines[2:]
        hid_bias = hid_of(vector[8 * width :])
        mixed_bias = jnp.concatenate([query_bias, jnp.zeros_like(query_bias), value_bias])
        mixed_bias = jnp.pad(mixed_bias, (0, mixed_rows - mixed_bias.shape[0]))
        return gains, biases, hid_bias, mixed_bias

    def enter(layer, value):
        gains, biases, _, _ = parameters(layer)
        normed = (norm_stats(value, mask, width)[0] * gains[0] + biases[0]).astype(BF)
        return gather_near(normed, n)

    def mix(layer, normed, w_attn, *others):
        mixed_bias = parameters(layer)[3]
        if fast and others:
            mixed_bias = tie(mixed_bias, *others)
        return (dot(w_attn, normed, (0, 1)) + mixed_bias[:, None]).astype(BF)

    def forward(layer, value, normed, mixed, w_proj, hold):
        gains, biases, hid_bias, _ = parameters(layer)
        proj_bias = tie(biases[3], fc_got[0]) if fast and layer == 0 else biases[3]
        attended, lse = attend(mixed, bias, slots, fast)
        if layer == 0:
            w_proj.append(get_proj(0, near, lse))
        w_proj = w_proj[layer]
        attended = heads_to_tokens(attended)
        middle = value + dot(attended, w_proj, (0, 0)) + proj_bias
        gain = hold(gains[1])
        normed_two = (norm_stats(middle, mask, width)[0] * gain + biases[4]).astype(BF)
        w_in, w_out = get_fc(layer, normed_two)
        normed_two = gather(normed_two, n)
        activated, slope = gelu_pair(dot(normed_two, w_in, (1, 0)) + hid_bias)
        activated, slope = lax.optimization_barrier((activated.astype(BF), slope.astype(BF)))
        kept = (value, normed, mixed, lse, attended, middle, normed_two, activated, slope)
        return kept, (w_in, w_out)

    def leave(layer, middle, activated, w_out):
        return dot(activated, w_out, (1, 0)).astype(BF)

    ones = lax.optimization_barrier(jnp.ones((16, length), BF))

    def backward(layer, grad_out, grad_low, kept, weights, fillers):
        value, normed, mixed, lse, attended, middle, normed_two, activated, slope = kept
        w_attn, w_proj, w_in, w_out = weights
        gains = parameters(layer)[0]
        low_sum = jnp.sum(grad_out, axis=0)
        grad_pre = (dot(grad_low, w_out, (1, 1)) * slope).astype(BF)
        part = dot(grad_pre, w_in, (1, 1)).astype(BF)
        fillers[0](part)
        grad_two = scatter(part)
        if fast:
            sent = dot(pick(activated, normed_two), pick(grad_low, grad_pre), (0, 0))
            sent = cross(sent.astype(BF))
            fc_pair = (pick(normed_two, activated), pick(grad_pre, grad_low), sent)
        else:
            fc_pair = (
                dot(normed_two, grad_pre, (0, 0)).astype(BF),
                dot(activated, grad_low, (0, 0)).astype(BF),
            )
        fillers[1](part)
        hid_sum = dot(ones, grad_pre, (1, 0))[0]
        gain = fillers[4](gains[1])
        grad_norm, gain_two, shift_two = norm_back(grad_two, middle, gain, mask, width)
        grad_middle = grad_out + grad_norm
        grad_branch = grad_middle.astype(BF)
        branch_sum = jnp.sum(grad_branch.astype(F32), axis=0)
        grad_attended = dot(w_proj, grad_branch, (1, 1)).astype(BF)
        grad_attended = tokens_to_heads(grad_attended)
        own, other = halves(grad_branch, proj_half, 1)
        if fast:
            sent = cross(dot(attended, other, (1, 0)).astype(BF))
            fc_total = (dot(fc_pair[0], fc_pair[1], (0, 0)) + fc_pair[2]).astype(BF)
            proj_total = (dot(attended, own, (1, 0)) + sent).astype(BF)
        else:
            fc_total = fc_pair
            proj_total = dot(attended, grad_branch, (1, 0)).astype(BF)
        fillers[2](grad_attended[-1], fc_total, proj_total)
        lse = fillers[3](lse, proj_total)
        grad_mixed = attend_back(mixed, grad_attended, bias, lse, slots, fast)
        part = dot(grad_mixed, w_attn, (0, 1)).astype(BF)
        grad_one = scatter(part)
        own, other = halves(grad_mixed, attn_half, 0)
        if fast:
            attn_pair = (own, cross(dot(normed, other, (0, 1)).astype(BF)))
            attn_total = (dot(normed, attn_pair[0], (0, 1)) + attn_pair[1]).astype(BF)
        else:
            attn_total = dot(normed, grad_mixed, (0, 1)).astype(BF)
        mixed_sum = jnp.sum(grad_mixed.astype(F32), axis=1)
        gain = fillers[5](gains[0])
        grad_norm, gain_one, shift_one = norm_back(grad_one, value, gain, mask, width)
        grad_in = grad_middle + grad_norm
        query_sum = heads_into(mixed_sum[:heads_width])
        value_sum = heads_into(mixed_sum[2 * heads_width : 3 * heads_width])
        lines = dense(
            jnp.stack([gain_one, gain_two, shift_one, branch_sum, shift_two, low_sum])
        )
        small = jnp.concatenate(
            [
                lines[:3].ravel(),
                query_sum,
                value_sum,
                lines[3:].ravel(),
                hid_into(hid_sum),
            ]
        )
        return grad_in, small, fc_total, proj_total, attn_total, grad_mixed

    if fast:

        proj_cut = (slab // 32) * 16

        def over_planes(total):
            return lax.psum_scatter(total, "seq", scatter_dimension=0, tiled=True)

        def both(mine_0, mine_1):
            return (mine_0, cross(mine_0, [(1, 0)])), (mine_1, cross(mine_1, [(0, 1)]))

        def finish(kernel, pairs, shape):
            (mine_0, other_0), (mine_1, other_1) = pairs
            choices = [(mine_0, other_1), (other_0, mine_1)]
            return chosen_call(kernel, section, choices, jax.ShapeDtypeStruct(shape, F32))

        def finish_fc(pairs):
            (mine_0, other_0), (mine_1, other_1) = pairs
            w_in = chosen_call(
                partial(finish_in_kernel, cut, padded),
                section,
                [(mine_0, other_1)],
                jax.ShapeDtypeStruct((rows, hidden), F32),
            )
            w_out = chosen_call(
                partial(finish_out_kernel, cut, padded),
                section,
                [(other_0, mine_1)],
                jax.ShapeDtypeStruct((hid, width), F32),
            )
            return w_in, w_out

        def reduce_small(small):
            total = pick(small[0], small[1]) + cross(pick(small[1], small[0]))
            total = total.reshape(-1, 128)
            out = [jax.ShapeDtypeStruct(total.shape, F32)]
            total = kernel_call(total_kernel, member, turned([total] * 4, "replica"), out)[0]
            total = kernel_call(total_kernel, plane, turned([total] * 4, "seq"), out)[0]
            return total.reshape(-1)

    held = {}

    def nothing(*_):
        pass

    def same(value, *_):
        return value

    values = source.astype(F32)
    fetch_proj(source)
    normed, near = enter(0, values)
    fetch_fc(0, near)
    attn_weights = [get_attn(0, source)]
    cotangent = to_team(cotangent)
    mixed = mix(0, normed, attn_weights[0], cotangent)
    proj_weights = []
    fetch_attn(mixed)
    fetch_fc(1, mixed)
    kept_0, fc_0 = forward(0, values, normed, mixed, proj_weights, same)
    part = leave(0, kept_0[5], kept_0[7], fc_0[1])
    attn_weights.append(get_attn(1, part))
    passed = kept_0[5] + scatter(part) + parameters(0)[1][5]
    values = passed.astype(BF).astype(F32)
    normed, near = enter(1, values)
    mixed = mix(1, normed, attn_weights[1])
    proj_weights.append(get_proj(1))
    grad_low = gather_late(tie(cotangent, edge_of(mixed)) if fast else cotangent)

    def hold_low(value):
        return value

    kept_1, fc_1 = forward(1, values, normed, mixed, proj_weights, hold_low)
    weights_0 = (attn_weights[0], proj_weights[0], *fc_0)
    weights_1 = (attn_weights[1], proj_weights[1], *fc_1)

    def finish_forward(part):
        held["out"] = scatter_late(leave(1, kept_1[5], kept_1[7], fc_1[1]))

    def start_fc(layer):
        def start(grad_attended, fc_total, proj_total):
            if fast:
                held[layer] = over_planes(fc_total)

        return start

    fillers = (nothing, finish_forward, start_fc(1), same, same, same)
    grad, small_1, fc_1, proj_1, attn_1, _ = backward(
        1, cotangent.astype(F32), grad_low, kept_1, weights_1, fillers
    )
    out = (kept_1[5] + held["out"] + parameters(1)[1][5]).astype(BF)
    grad = grad.astype(BF)
    grad_low = gather(grad, n)
    fillers = (nothing, nothing, start_fc(0), same, same, same)
    if fast:
        attn_1 = over_planes(attn_1)

        held["fc_1"] = lax.all_gather(held[1], "replica", axis=0, tiled=True)

        held["attn_1"] = lax.all_gather(attn_1, "replica", axis=0, tiled=True)

        def hold_sums(value, proj_0):
            held["proj"] = whole = jnp.concatenate([proj_0, proj_1], axis=1)
            held["got"] = scatter_first(whole)
            return tie(value, *held["got"])

        def hold_attn(value):
            return tie(value, held["attn_1"])

        def hold_gathered(value):
            return tie(value, held["fc_1"])

        fillers = (nothing, nothing, start_fc(0), hold_sums, hold_gathered, hold_attn)
    grad, small_0, fc_0, proj_0, attn_0, grad_mixed = backward(
        0, grad.astype(F32), grad_low, kept_0, weights_0, fillers
    )
    grad = grad.astype(BF)
    if fast:
        proj = scatter(held["proj"], held["got"]).astype(BF)
        proj = over_planes(proj)
        attn_last = attn_0
        attn_0 = over_planes(attn_0)
        mine = from_team(jnp.concatenate([grad, out], axis=1))
        edge = kernel_call(
            partial(edge_kernel, padded),
            section,
            [mine, cross(mine)],
            [jax.ShapeDtypeStruct((1, 2, 1, local, width), F32)],
        )[0]
        fc_0 = lax.all_gather(tie(held[0], edge_of(attn_last)), "replica", axis=0, tiled=True)
        fc = both(fc_0, held["fc_1"])
        attn = both(gather_direct(attn_0)[0], held["attn_1"])
        proj = both(*gather_direct(proj, [proj_half, proj_half]))
    else:
        out, grad = from_team(out), from_team(grad)
        got_out, got_grad = cross(out, [(0, 1)]), cross(grad, [(1, 0)])
        edge = jnp.stack([pick(grad, got_out), pick(got_grad, out)]).astype(F32)
    edge = edge.reshape(1, 2, 1, local, width)
    if fast:
        in_sum, out_sum = finish_fc(fc)
        kernel = partial(finish_proj_kernel, step, slab, proj_cut, wide, padded)
        proj_sum = finish(kernel, proj, (rows, width))
        kernel = partial(finish_attn_kernel, slots, cut, mixed_rows)
        attn_sum = finish(kernel, attn, (rows, 3 * width))
        small = reduce_small((small_0, small_1))
    else:

        def summed(make, after):
            parts = [lax.optimization_barrier((make(layer), after))[0] for layer in range(2)]
            mine = pick(parts[0], parts[1]) + cross(pick(parts[1], parts[0]))
            mine = lax.psum_scatter(mine, row_axes, scatter_dimension=0, tiled=True)
            return lax.psum(mine.astype(F32), ("replica",))

        def attn_whole(layer):
            value = (attn_0, attn_1)[layer]
            zeros = jnp.zeros((width, width), BF)
            parts = [value[:, i * heads_width : (i + 1) * heads_width] for i in range(3)]
            return jnp.concatenate(
                [lax.dynamic_update_slice_in_dim(zeros, x, start, 1) for x in parts], axis=1
            )

        def proj_whole(layer):
            return (proj_0, proj_1)[layer]

        def in_whole(layer):
            zeros = jnp.zeros((width, hidden), BF)
            part = (fc_0, fc_1)[layer][0]
            return lax.dynamic_update_slice_in_dim(zeros, part, member * hid, 1)

        def out_whole(layer):
            zeros = jnp.zeros((hidden, width), BF)
            part = (fc_0, fc_1)[layer][1]
            return lax.dynamic_update_slice_in_dim(zeros, part, member * hid, 0)

        attn_sum = summed(attn_whole, edge)
        proj_sum = summed(proj_whole, attn_sum)
        in_sum = summed(in_whole, proj_sum)
        out_sum = summed(out_whole, in_sum)
        small = pick(small_0, small_1) + cross(pick(small_1, small_0))
        small = lax.psum(small, chip_axes)
    return (
        edge,
        attn_sum[None],
        proj_sum[None],
        in_sum[None],
        out_sum[None],
        small[: 2 * width].reshape(1, 2, width),
        small[2 * width : 8 * width].reshape(1, 6, width),
        small[8 * width :][None],
    )


def solution(mesh):
    sections, replicas, shards = (mesh.shape[name] for name in ("section", "replica", "shard"))
    split = Mesh(
        mesh.devices.reshape(sections, replicas, replicas, shards // replicas),
        ("section", "replica", "seq", "sub"),
    )
    rows = ("seq", "sub")
    return jax.shard_map(
        partial(body, replicas, shards),
        mesh=split,
        in_specs=(
            P("section", None, "replica", rows, None),
            P(None, "replica", None),
            P("section", rows, None),
            P("section", rows, None),
            P("section", rows, None),
            P("section", rows, None),
            P("section", None, None),
            P("section", None, None),
            P("section", None),
        ),
        out_specs=(
            P("section", None, "replica", rows, None),
            P("section", rows, None),
            P("section", rows, None),
            P("section", rows, None),
            P("section", rows, None),
            P("section", None, None),
            P("section", None, None),
            P("section", None),
        ),
        check_vma=False,
    )
```
